32 devices in a mesh: grp: 4 (over y, x), fsdp: 8 (over z, core).
Axes of the slice: x: 2, y: 2, z: 4, core: 2. Of those that a mesh axis runs over, the one named last changes fastest.
Arguments:
- hidden: bfloat16 [64, 257, 1024], P(('grp', 'fsdp')), may hold values from -6 to 6
- ln1_gain: float32 [1024], replicated, may hold values from 0.25 to 1.75
- w_qkv: bfloat16 [1024, 3072], P('fsdp'), may hold values from -0.1875 to 0.1875
- w_out: bfloat16 [1024, 1024], P('fsdp'), may hold values from -0.1875 to 0.1875
- ln2_gain: float32 [1024], replicated, may hold values from 0.25 to 1.75
- w_up: bfloat16 [1024, 4096], P('fsdp'), may hold values from -0.1875 to 0.1875
- w_down: bfloat16 [4096, 1024], P('fsdp'), may hold values from -0.09375 to 0.09375
- post_gain: float32 [1024], replicated, may hold values from 0.25 to 1.75
- w_proj: bfloat16 [1024, 256], replicated, may hold values from -0.1875 to 0.1875
- table: float32 [32, 2048, 256], P(('grp', 'fsdp')), may hold values from -6 to 6
- accum: float32 [32, 2048, 256], P(('grp', 'fsdp')), may hold values from 0.1 to 4
- place: int32 [32], replicated, may hold values from 0 to 31, each once
- lookup_table: int32 [4096, 1], P(('grp', 'fsdp')), may hold values from 0 to 31; in each aligned block of 128 rows (0 to 127, 128 to 255, ...) at most 8 rows name the same one
- lookup_row: int32 [4096], P(('grp', 'fsdp')), may hold values from 0 to 2047
Outputs:
- table_new: float32 [32, 2048, 256], P(('grp', 'fsdp'))
- accum_new: float32 [32, 2048, 256], P(('grp', 'fsdp'))
- content_grad: float32 [64, 256], P(('grp', 'fsdp'))
- proj_grad: float32 [1024, 256], P(('grp', 'fsdp'))
The draws below stay inside these ranges and needn't reach their ends.
Inputs may be any that keep to these rules, and one draw needn't show every extreme that they name: `lookup_table`: within the lookups of one device (aligned blocks of 128), no table is named more than 8 times, a bound that some block reaches. `place`: every device holds exactly one table.
All inputs are finite; a program needn't handle non-finite values.
Results may differ from the reference program's by a relative error of at most 0.0044.
Values may be sent and summed in bfloat16 or wider, within the bound.
No kernel may reach another device: no remote copies, remote signals or barrier semaphores. Data moves between devices by JAX's collectives and lax.ppermute only.
A program may use at most 192 MiB of HBM per device.

```python
import math
import jax
import jax.numpy as jnp
import numpy as np
from jax import lax

D = 1024
HEADS = 16
MLP = 4096
SEQ = 257
PROJ = 256
LOOK_IMG = 64
ROWS_DEV = 2048
LOOK_DEV = 128
TABLES = 32
CAP = 8
IMAGES = 64
LOOKUPS = 4096
DEVICES = 32


def place_ends(entries, rng, low, top_value):
    spot = [jax.random.randint(jax.random.fold_in(rng, axis), (), 0, length) for axis, length in enumerate(entries.shape)]
    main_axis = entries.shape.index(max(entries.shape))
    neighbour = spot[:main_axis] + [(spot[main_axis] + 1) % entries.shape[main_axis]] + spot[main_axis + 1:]
    return entries.at[tuple(spot)].set(low).at[tuple(neighbour)].set(top_value)


def steps_of(rng, shape, pieces, smallest, high):
    level, own = 1.0, jax.random.fold_in(rng, 6)
    for axis_at, blocks in pieces:
        heights = jnp.exp(jax.random.uniform(jax.random.fold_in(own, axis_at), (blocks,), jnp.float32, smallest / len(pieces), high / len(pieces)))
        level = level * jnp.repeat(heights, shape[axis_at] // blocks).reshape([-1 if axis == axis_at else 1 for axis in range(len(shape))])
    return level


def deal_out(stream_key, own, number, rows, number_of, top, reach, skew):
    sequence = jax.random.permutation(stream_key, number_of)
    heavy_load, usual = portions_of(number_of, rows * top, reach, skew, True), portions_of(number_of, rows * top, reach, skew, False)
    places = jnp.arange(number_of)

    def named(sizes, turn):
        used = int((sizes > 0).sum())
        fixed = max(1, used // 4)
        moved = fixed + (places - fixed + turn * (used - fixed)) % max(1, number_of - fixed)
        return jnp.zeros((number_of,), jnp.int32).at[sequence[jnp.where(places < fixed, places, moved)]].set(jnp.asarray(sizes, jnp.int32))

    sizes = jnp.where(number % 4 == 0, named(heavy_load, number // 4), named(usual, number - number // 4 - 1))
    mixed = jax.random.permutation(jax.random.fold_in(own, 3), number_of)
    source_of, taker = mixed[0:number_of // 2 * 2:2], mixed[1:number_of // 2 * 2:2]
    margin = jnp.minimum(sizes[source_of] - 1, reach - sizes[taker]) // 2
    margin = jnp.where((source_of == sequence[0]) | (taker == sequence[0]) | (sizes[taker] == 0), 0, jnp.maximum(margin, 0))
    moved = jax.random.randint(jax.random.fold_in(own, 4), (number_of // 2,), 0, 1 << 20) % (margin + 1)
    sizes = sizes.at[source_of].add(-moved).at[taker].add(moved)
    labels = jnp.searchsorted(jnp.cumsum(sizes), jnp.arange(rows * top), side="right").astype(jnp.int32)
    listing = labels.reshape(top, rows).T
    listing = listing[jax.random.permutation(jax.random.fold_in(own, 1), rows)]
    turn = jax.random.randint(jax.random.fold_in(own, 2), (rows, 1), 0, top)
    return jnp.take_along_axis(listing, (jnp.arange(top)[None, :] + turn) % top, axis=1)


def portions_of(count, total, bound, slope, full):
    weights = [(1 << 20) // math.isqrt(standing ** slope) + 1 for standing in range(1, count + 1)]
    largest = bound if full else min(bound, max(-(-total // count), total * weights[0] // sum(weights)))
    least = 1 if total - largest >= count - 1 else 0
    given, spare = [largest] + [least] * (count - 1), total - largest - least * (count - 1)
    while spare > 0:
        candidates = [i for i in range(1, count) if given[i] < largest] or [i for i in range(1, count) if given[i] < bound]
        pool, budget = sum([weights[i] for i in candidates]), spare
        for i in candidates:
            extra = min(bound - given[i], max(1, budget * weights[i] // pool), spare)
            given[i] = given[i] + extra
            spare = spare - extra
    return np.array(given)


def bell_draw(own_key, dims, deviation, reach, pieces=(), kind=jnp.bfloat16):
    result = jax.random.normal(own_key, dims, jnp.float32) * deviation
    if len(pieces) > 0:
        result = steps_of(own_key, dims, pieces, -0.22, 0.18) * result
    return jnp.clip(result, min=-reach, max=reach).astype(kind)


def setup_inputs(seed: int = 0) -> dict:
    streams_of = jax.random.split(jax.random.key(seed), 15)
    hidden = bell_draw(streams_of[0], (IMAGES, SEQ, D), 1.0, 6.0, ((0, 32),))
    ln1_gain = jnp.clip(1.0 + 0.15 * jax.random.normal(streams_of[1], (D,), jnp.float32), 0.25, 1.75)
    w_qkv = bell_draw(streams_of[2], (D, 3 * D), D ** -0.5, 0.1875, ((0, 8),))
    w_out = bell_draw(streams_of[3], (D, D), D ** -0.5, 0.1875, ((0, 8),))
    ln2_gain = jnp.clip(1.0 + 0.15 * jax.random.normal(streams_of[4], (D,), jnp.float32), 0.25, 1.75)
    w_up = bell_draw(streams_of[5], (D, MLP), D ** -0.5, 0.1875, ((0, 8),))
    w_down = bell_draw(streams_of[6], (MLP, D), MLP ** -0.5, 0.09375, ((0, 8),))
    post_gain = jnp.clip(1.0 + 0.15 * jax.random.normal(streams_of[7], (D,), jnp.float32), 0.25, 1.75)
    w_proj = bell_draw(streams_of[8], (D, PROJ), D ** -0.5, 0.1875)
    table = bell_draw(streams_of[9], (DEVICES, ROWS_DEV, PROJ), 1.0, 6.0, ((0, 32),), jnp.float32)
    accum = jnp.clip(jnp.exp(math.log(4.0) - 3.6888794 * jax.random.uniform(streams_of[10], (DEVICES, ROWS_DEV, PROJ), jnp.float32) ** steps_of(streams_of[10], (DEVICES, ROWS_DEV, PROJ), ((0, 32),), -0.2, 0.2)), 0.1, 4.0)
    place = jax.random.permutation(streams_of[11], TABLES).astype(jnp.int32)
    lookup_table_keys = jax.random.split(jax.random.fold_in(streams_of[12], 1), LOOKUPS // LOOK_DEV)
    lookup_table_turns = jax.random.permutation(jax.random.fold_in(streams_of[12], 3), LOOKUPS // LOOK_DEV)
    lookup_table = jax.vmap(lambda own, number: deal_out(jax.random.fold_in(streams_of[12], 2), own, number, LOOK_DEV, TABLES, 1, CAP, 2))(lookup_table_keys, lookup_table_turns).reshape((LOOKUPS, 1))
    lookup_row = place_ends(jax.random.randint(streams_of[13], (LOOKUPS,), 0, ROWS_DEV), jax.random.fold_in(streams_of[13], 1), 0, ROWS_DEV - 1).astype(jnp.int32)
    return {"hidden": hidden, "ln1_gain": ln1_gain, "w_qkv": w_qkv, "w_out": w_out, "ln2_gain": ln2_gain, "w_up": w_up, "w_down": w_down, "post_gain": post_gain, "w_proj": w_proj, "table": table, "accum": accum, "place": place, "lookup_table": lookup_table, "lookup_row": lookup_row}


epsilon = 1e-06
learn_rate = 0.5

def layer_norm(values, gain):
    center = lax.optimization_barrier(jnp.mean(values, axis=-1, keepdims=True))
    shifted = values - center
    spread = lax.optimization_barrier(jnp.mean(shifted * shifted, axis=-1, keepdims=True))
    return shifted * lax.rsqrt(spread + epsilon) * gain.astype(jnp.float32)

def encode_block(block, ln1_gain, w_qkv, w_out, ln2_gain, w_up, w_down, post_gain):
    images, seq, width = block.shape
    head_dim = width // HEADS
    tokens = block.reshape(images * seq, width)
    normed = layer_norm(tokens.astype(jnp.float32), ln1_gain).astype(jnp.bfloat16)
    qkv = jnp.dot(normed, w_qkv, preferred_element_type=jnp.float32).astype(jnp.bfloat16)
    qkv = qkv.reshape(images, seq, 3, HEADS, head_dim)
    query = qkv[:, :, 0].astype(jnp.float32)
    keys = qkv[:, :, 1].astype(jnp.float32)
    values = qkv[:, :, 2].astype(jnp.float32)
    scores = jnp.einsum('bqhd,bkhd->bhqk', query, keys) / math.sqrt(head_dim)
    probs = jax.nn.softmax(scores, axis=-1).astype(jnp.bfloat16)
    mixed = jnp.einsum('bhqk,bkhd->bqhd', probs.astype(jnp.float32), values)
    mixed = mixed.astype(jnp.bfloat16).reshape(images * seq, width)
    resid = tokens.astype(jnp.float32) + jnp.dot(mixed, w_out, preferred_element_type=jnp.float32)
    resid = resid.astype(jnp.bfloat16)
    normed_two = layer_norm(resid.astype(jnp.float32), ln2_gain).astype(jnp.bfloat16)
    upward = jnp.dot(normed_two, w_up, preferred_element_type=jnp.float32)
    active = jax.nn.gelu(upward, approximate=False).astype(jnp.bfloat16)
    final = resid.astype(jnp.float32) + jnp.dot(active, w_down, preferred_element_type=jnp.float32)
    posted = layer_norm(final, post_gain).reshape(images, seq, width)
    return lax.optimization_barrier(jnp.mean(posted, axis=1)).astype(jnp.bfloat16)

def reference(hidden, ln1_gain, w_qkv, w_out, ln2_gain, w_up, w_down, post_gain, w_proj, table, accum, place, lookup_table, lookup_row):
    blocks = hidden.reshape(-1, 8, SEQ, D)

    def encode_one(block):
        return encode_block(block, ln1_gain, w_qkv, w_out, ln2_gain, w_up, w_down, post_gain)
    pooled = lax.map(encode_one, blocks).reshape(-1, D)
    content = jnp.dot(pooled, w_proj, preferred_element_type=jnp.float32)
    scale = lax.rsqrt(lax.optimization_barrier(jnp.mean(content * content, axis=-1, keepdims=True)) + epsilon)
    unit = content * scale
    owner = place[lookup_table[:, 0]].astype(jnp.int32)
    flat = (owner * ROWS_DEV + lookup_row).astype(jnp.int32)
    flat_table = table.reshape(-1, PROJ)
    diff = flat_table[flat] - jnp.repeat(unit, LOOK_IMG, axis=0)
    grad_rows = jnp.zeros(flat_table.shape, jnp.float32).at[flat].add(diff)
    accum_new = accum.reshape(-1, PROJ) + grad_rows * grad_rows
    table_new = flat_table - learn_rate * grad_rows / jnp.sqrt(accum_new)
    grad_unit = -lax.optimization_barrier(jnp.sum(diff.reshape(-1, LOOK_IMG, PROJ), axis=1))
    inner = lax.optimization_barrier(jnp.mean(grad_unit * unit, axis=-1, keepdims=True))
    content_grad = scale * (grad_unit - unit * inner)
    proj_grad = jnp.dot(pooled.astype(jnp.float32).T, content_grad, precision=lax.Precision.HIGHEST, preferred_element_type=jnp.float32)
    return (table_new.reshape(table.shape), accum_new.reshape(accum.shape), content_grad, proj_grad)
```

```python
import functools
import math

import jax
import jax.numpy as jnp
from jax import lax
from jax.experimental import pallas as pl
from jax.experimental.pallas import tpu as pltpu
from jax.sharding import PartitionSpec as P

HEADS = 16
LOOK_IMG = 64
CORES = 2
LANES = 128
MIB = 1 << 20

epsilon = 1e-06
learn_rate = 0.5
bf16 = jnp.bfloat16
f32 = jnp.float32
BOTH = ("grp", "fsdp")

VMEM = pl.BlockSpec(memory_space=pltpu.VMEM)
SMEM = pl.BlockSpec(memory_space=pltpu.SMEM)
ANY = pl.BlockSpec(memory_space=pl.ANY)


def norm_rows(values, gain):
    center = jnp.mean(values, axis=-1, keepdims=True)
    shifted = values - center
    spread = jnp.mean(shifted * shifted, axis=-1, keepdims=True)
    return shifted * lax.rsqrt(spread + epsilon) * gain


def spread_shards(shards, grp, fsdp, turn):
    chips = fsdp // CORES
    both = tuple(BOTH)

    def moved(value, target):
        pairs = []
        for index in range(grp * fsdp):
            plane, rest = divmod(index, fsdp)
            chip, core = divmod(rest, CORES)
            there = target(plane, chip, core)
            pairs.append((index, (there[0] * chips + there[1]) * CORES + there[2]))
        return lax.ppermute(value, both, pairs)

    def swap(value, bit):
        return moved(value, lambda g, c, k: (g ^ bit, c, k))

    def sibling(value):
        return moved(value, lambda g, c, k: (g, c, k ^ 1))

    part = jnp.concatenate(
        [
            lax.dynamic_slice_in_dim(s, turn * (s.shape[1] // grp), s.shape[1] // grp, axis=1)
            for s in shards
        ],
        axis=1,
    )
    along = [
        moved(part, lambda g, c, k, step=step: (g, (c - step) % chips, k))
        for step in range(1, chips)
    ]
    mine = jnp.concatenate(along, axis=0)
    one, two = swap(mine, 1), swap(mine, 2)
    half = mine.shape[0] // 2
    low, high = swap(one[:half], 2), swap(two[half:], 1)
    sent = [mine, one, two, low, high]
    return sent, [sibling(v) for v in sent], [sibling(s) for s in shards]


def piece_plan(chips, rows, wide, offset):
    plan = []
    half = (chips - 1) * rows // 2
    for turn in range(3):
        for step in range(1, chips):
            for side in range(2):
                plan.append((1 + turn, (step - 1) * rows, rows, offset, side, step, 0, turn))
    for step in range(1, chips):
        for side in range(2):
            first, last = (step - 1) * rows, step * rows
            for buffer, low, high, base in ((4, 0, half, 0), (5, half, 2 * half, half)):
                start, stop = max(first, low), min(last, high)
                if start < stop:
                    plan.append(
                        (buffer, start - base, stop - start, offset, side, step, start - first, 3)
                    )
    return plan


class Weight:
    def __init__(self, shape, wide, pieces, plan, chips, rows):
        self.shape, self.wide, self.pieces = shape, wide, pieces
        self.plan, self.chips, self.rows = plan, chips, rows

    @property
    def count(self):
        return len(self.pieces)

    @property
    def copies(self):
        return 1 if self.plan is None else 2 + len(self.plan)

    def start(self, refs, whole, sems, pos):
        if self.plan is None:
            copy = pltpu.make_async_copy(refs[0], whole, sems.at[0])
            copy.start()
            return [[copy], [], [], []]
        plane, chip, core = pos[0], pos[1], pos[2]
        groups = [[], [], [], []]
        number = 0

        def go(source, target, turn):
            nonlocal number
            copy = pltpu.make_async_copy(source, target, sems.at[number])
            copy.start()
            groups[turn].append(copy)
            number += 1

        for side in range(2):
            row = pl.multiple_of((chip * CORES + (core ^ side)) * self.rows, self.rows)
            go(refs[side * 6], whole.at[pl.ds(row, self.rows), :], 0)
        for buffer, low, count, column, side, step, inner, turn in self.plan:
            there = lax.rem(chip + step, self.chips)
            row = (there * CORES + (core ^ side)) * self.rows + inner
            row = pl.multiple_of(row, math.gcd(self.rows, inner) if inner else self.rows)
            left = pl.multiple_of((plane ^ turn) * self.wide, LANES)
            go(
                refs[side * 6 + buffer].at[pl.ds(low, count), pl.ds(column, self.wide)],
                whole.at[pl.ds(row, count), pl.ds(left, self.wide)],
                turn,
            )
        return groups

    def each_turn(self, refs, whole, sems, pos, body):
        groups = self.start(refs, whole, sems, pos)
        for turn in range(4):
            for copy in groups[turn]:
                copy.wait()
            left = (pos[0] ^ turn) * self.wide if self.plan is not None else turn * self.wide
            body(left)


def gather_chunks(chunks, grp, fsdp, turn):
    found = []
    chips = fsdp // CORES
    for shards in chunks:
        rows = shards[0].shape[0]
        simple = grp == 4 and fsdp % CORES == 0 and rows % LANES == 0 and chips % 2 == 0
        if simple:
            sent, other, other_own = spread_shards(shards, grp, fsdp, turn)
        offset = 0
        for number, shard in enumerate(shards):
            wide = shard.shape[1] // 4
            shape = (rows * fsdp, shard.shape[1])
            if simple:
                pieces = [shard] + sent + [other_own[number]] + other
                plan = piece_plan(chips, rows, wide, offset)
            else:
                pieces, plan = [lax.all_gather(shard, "fsdp", axis=0, tiled=True)], None
            offset += wide
            found.append(Weight(shape, wide, pieces, plan, chips, rows))
    return found


def block_of(wide):
    return 256 if wide % 256 == 0 else LANES


def call_with_weight(weight, body, pos, inputs, out_shapes, scratch, room, flops, name):
    n_in, n_out = len(inputs), len(out_shapes)

    def kernel(*refs):
        pos_ref = refs[0]
        pieces = refs[1 : 1 + weight.count]
        refs = refs[1 + weight.count :]
        ins, outs, rest = refs[:n_in], refs[n_in : n_in + n_out], refs[n_in + n_out :]
        whole, sems = rest[0], rest[1]

        def each_turn(work):
            weight.each_turn(pieces, whole, sems, pos_ref, work)

        body(ins, outs, rest[2:], whole, each_turn)

    return pl.pallas_call(
        kernel,
        out_shape=out_shapes,
        in_specs=[SMEM] + [ANY] * weight.count + [VMEM] * n_in,
        out_specs=[VMEM] * n_out,
        scratch_shapes=[
            pltpu.VMEM(weight.shape, bf16),
            pltpu.SemaphoreType.DMA((weight.copies,)),
        ]
        + list(scratch),
        compiler_params=pltpu.CompilerParams(vmem_limit_bytes=room * MIB),
        cost_estimate=pl.CostEstimate(flops=flops, bytes_accessed=2 * math.prod(weight.shape), transcendentals=0),
        name=name,
    )(pos, *weight.pieces, *inputs)


def dot32(left, right):
    return jnp.dot(left, right, preferred_element_type=f32)


def column_loop(wide, left, work):
    size = block_of(wide)

    @pl.loop(0, wide // size)
    def _(number):
        work(pl.ds(pl.multiple_of(left + number * size, LANES), size))


def project_qkv(weight, pos, normed):
    def body(ins, outs, scratch, whole, each_turn):
        def quarter(left):
            def work(columns):
                outs[0][:, columns] = dot32(ins[0][...], whole[:, columns]).astype(bf16)

            column_loop(weight.wide, left, work)

        each_turn(quarter)

    rows = normed.shape[0]
    return call_with_weight(
        weight, body, pos, [normed],
        [jax.ShapeDtypeStruct((rows, weight.shape[1]), bf16)], [], 24,
        2 * rows * math.prod(weight.shape), "project_qkv",
    )[0]


def attend(qkv, images, padded, seq, width):
    head_dim = width // HEADS
    per = LANES // head_dim
    blocks = width // LANES
    factor = 1.0 / (math.sqrt(head_dim) * math.log(2.0))

    def kernel(query, keys, values, out):
        q, k, v = query[0], keys[0], values[0]
        lane = lax.broadcasted_iota(jnp.int32, (1, LANES), 1)
        column = lax.broadcasted_iota(jnp.int32, (1, padded), 1)
        beside = jnp.concatenate([v, jnp.ones_like(v)], axis=1)
        total = None
        for head in range(per):
            own = (lane // head_dim) == head
            scores = lax.dot_general(
                jnp.where(own, q, jnp.zeros_like(q)), k,
                (((1,), (1,)), ((), ())), preferred_element_type=f32,
            )
            scores = jnp.where(column < seq, scores, -1e30)
            top = jnp.max(scores, axis=-1, keepdims=True)
            probs = jnp.exp2((scores - top) * factor).astype(bf16)
            both = dot32(probs, beside)
            mixed = both[:, :LANES] / both[:, LANES:]
            total = mixed if total is None else jnp.where(own, mixed, total)
        out[0] = total.astype(bf16)

    spec = lambda shift: pl.BlockSpec((1, padded, LANES), lambda i, h: (i, 0, h + shift * blocks))
    shaped = qkv.reshape(images, padded, 3 * width)
    mixed = pl.pallas_call(
        kernel,
        grid=(images, blocks),
        out_shape=jax.ShapeDtypeStruct((images, padded, width), bf16),
        in_specs=[spec(0), spec(1), spec(2)],
        out_specs=spec(0),
        compiler_params=pltpu.CompilerParams(vmem_limit_bytes=16 * MIB),
        cost_estimate=pl.CostEstimate(
            flops=8 * images * padded * padded * width, bytes_accessed=8 * images * padded * width,
            transcendentals=images * HEADS * padded * padded,
        ),
        name="attend",
    )(shaped, shaped, shaped)
    return mixed.reshape(images * padded, width)


def project_out(weight, pos, mixed, tokens, gain):
    rows, width = mixed.shape

    def body(ins, outs, scratch, whole, each_turn):
        mixed_ref, tokens_ref, gain_ref = ins
        resid, normed = outs

        def quarter(left):
            def work(columns):
                product = dot32(mixed_ref[...], whole[:, columns])
                resid[:, columns] = (tokens_ref[:, columns].astype(f32) + product).astype(bf16)

            column_loop(weight.wide, left, work)

        each_turn(quarter)
        step = 32 if rows % 32 == 0 else 16

        @pl.loop(0, rows // step)
        def _(number):
            at = pl.ds(pl.multiple_of(number * step, step), step)
            normed[at, :] = norm_rows(resid[at, :].astype(f32), gain_ref[...]).astype(bf16)

    shape = jax.ShapeDtypeStruct((rows, width), bf16)
    return call_with_weight(
        weight, body, pos, [mixed, tokens, gain.reshape(1, -1)], [shape, shape], [], 16,
        2 * rows * math.prod(weight.shape), "project_out",
    )


def gelu(values):
    return 0.5 * values * (1.0 + lax.erf(values * math.sqrt(0.5)))


def project_up(weight, pos, normed):
    rows = normed.shape[0]

    def body(ins, outs, scratch, whole, each_turn):
        def quarter(left):
            def work(columns):
                outs[0][:, columns] = gelu(dot32(ins[0][...], whole[:, columns])).astype(bf16)

            column_loop(weight.wide, left, work)

        each_turn(quarter)

    return call_with_weight(
        weight, body, pos, [normed],
        [jax.ShapeDtypeStruct((rows, weight.shape[1]), bf16)], [], 28,
        4 * rows * math.prod(weight.shape), "project_up",
    )[0]


def project_down(weight, pos, active, resid, gain, images, seq, devices):
    rows, width = resid.shape
    padded = rows // images

    def body(ins, outs, scratch, whole, each_turn):
        active_ref, resid_ref, gain_ref = ins
        (final,) = scratch
        (pooled,) = outs

        def quarter(left):
            def work(columns):
                product = dot32(active_ref[...], whole[:, columns])
                final[:, columns] = resid_ref[:, columns].astype(f32) + product

            column_loop(weight.wide, left, work)

        each_turn(quarter)
        step = 16
        for image in range(images):

            def add(number, total):
                at = pl.ds(pl.multiple_of(image * padded + number * step, step), step)
                posted = norm_rows(final[at, :], gain_ref[...])
                row = lax.broadcasted_iota(jnp.int32, (step, 1), 0) + number * step
                return total + jnp.where(row < seq, posted, 0.0)

            total = lax.fori_loop(0, padded // step, add, jnp.zeros((step, width), f32))
            mean = (jnp.sum(total, axis=0, keepdims=True) / seq).astype(bf16)
            for device in range(devices):
                pooled[device, image : image + 1, :] = mean

    return call_with_weight(
        weight, body, pos, [active, resid, gain.reshape(1, -1)],
        [jax.ShapeDtypeStruct((devices, images, width), bf16)],
        [pltpu.VMEM((rows, width), f32)], 32,
        2 * rows * math.prod(weight.shape), "project_down",
    )[0]


def thirds(values):
    first = values.astype(bf16)
    left = values - first.astype(f32)
    second = left.astype(bf16)
    return first, second, (left - second.astype(f32)).astype(bf16)


def update(pos, every, proj, sums, named, table, accum, images, share):
    rows, width = table.shape
    every_image, depth = every.shape
    blocks = rows // LANES
    per = 4 if blocks % 4 == 0 else 1
    side = max(share, LANES)
    over = (((0,), (0,)), ((), ()))

    def kernel(pos_ref, every_ref, proj_ref, sums_ref, named_ref, table_ref, accum_ref,
               table_out, accum_out, content_out, proj_out, units, grads, square):
        @pl.when(pl.program_id(0) == 0)
        def _():
            content = dot32(every_ref[...], proj_ref[...])
            scale = lax.rsqrt(jnp.mean(content * content, axis=-1, keepdims=True) + epsilon)
            unit = content * scale
            for number, part in enumerate(thirds(unit)):
                units[number * every_image : (number + 1) * every_image, :] = part
            grad_unit = LOOK_IMG * unit - sums_ref[...]
            inner = jnp.mean(grad_unit * unit, axis=-1, keepdims=True)
            grad = scale * (grad_unit - unit * inner)
            grads[...] = grad
            me = pos_ref[3]
            for image in range(images):
                content_out[image : image + 1, :] = grads[pl.ds(me * images + image, 1), :]
            column = me * share
            block = pl.multiple_of((column // side) * side, side)
            mine = every_ref[:, pl.ds(block, side)]
            total = None
            for part in thirds(grad):
                product = lax.dot_general(mine, part, over, preferred_element_type=f32)
                total = product if total is None else total + product
            square[...] = total
            unit_rows = math.gcd(share, side)
            proj_out[...] = square[pl.ds(pl.multiple_of(column - block, unit_rows), share), :]

        ones = jnp.ones((every_image, width), bf16)
        for number in range(per):
            at = slice(number * LANES, (number + 1) * LANES)
            count = named_ref[number]
            times = lax.dot_general(count, ones, over, preferred_element_type=f32)
            taken = None
            for part in range(3):
                product = lax.dot_general(
                    count, units[part * every_image : (part + 1) * every_image, :], over,
                    preferred_element_type=f32,
                )
                taken = product if taken is None else taken + product
            old = table_ref[at, :]
            grad_rows = times * old - taken
            grown = accum_ref[at, :] + grad_rows * grad_rows
            accum_out[at, :] = grown
            table_out[at, :] = old - learn_rate * grad_rows / jnp.sqrt(grown)

    whole = lambda shape: pl.BlockSpec(shape, lambda i: (0,) * len(shape))
    strip = pl.BlockSpec((per * LANES, width), lambda i: (i, 0))
    return pl.pallas_call(
        kernel,
        grid=(blocks // per,),
        out_shape=[
            jax.ShapeDtypeStruct(table.shape, f32),
            jax.ShapeDtypeStruct(table.shape, f32),
            jax.ShapeDtypeStruct((images, width), f32),
            jax.ShapeDtypeStruct((share, width), f32),
        ],
        in_specs=[
            SMEM, whole(every.shape), whole(proj.shape), whole(sums.shape),
            pl.BlockSpec((per, every_image, LANES), lambda i: (i, 0, 0)), strip, strip,
        ],
        out_specs=[strip, strip, whole((images, width)), whole((share, width))],
        scratch_shapes=[
            pltpu.VMEM((3 * every_image, width), bf16),
            pltpu.VMEM((every_image, width), f32),
            pltpu.VMEM((side, width), f32),
        ],
        compiler_params=pltpu.CompilerParams(vmem_limit_bytes=24 * MIB),
        name="update",
    )(pos, every, proj, sums, named, table, accum)


def broadcast_all(value, devices):
    return lax.all_to_all(
        jnp.broadcast_to(value[None], (devices,) + value.shape), BOTH, 0, 0, tiled=True
    )


def on_device(
    hidden, ln1_gain, w_qkv, w_out, ln2_gain, w_up, w_down, post_gain, w_proj,
    table, accum, place, lookup_table, lookup_row,
):
    images, seq, width = hidden.shape
    grp, fsdp = lax.axis_size("grp"), lax.axis_size("fsdp")
    devices = grp * fsdp
    plane, spot = lax.axis_index("grp"), lax.axis_index("fsdp")
    me = plane * fsdp + spot
    pos = jnp.stack([plane, spot // CORES, spot % CORES, me]).astype(jnp.int32)

    qkv_w, out_w, up_w, down_w = gather_chunks(
        [[w_qkv], [w_out, w_up], [w_down]], grp, fsdp, plane
    )

    rows_dev, proj_width = table.shape[1:]
    every_image = images * devices
    my_table = jnp.sum(jnp.where(place == me, jnp.arange(place.shape[0], dtype=jnp.int32), 0))
    both = jnp.stack([lookup_table[:, 0], lookup_row])
    named = broadcast_all(both, devices)
    tables = named[:, 0].reshape(every_image, LOOK_IMG)
    rows = named[:, 1].reshape(every_image, LOOK_IMG)
    high = jnp.where(tables == my_table, rows // LANES, -1)
    left = (high[:, :, None] == jnp.arange(rows_dev // LANES)[None, None, :]).astype(bf16)
    right = ((rows % LANES)[:, :, None] == jnp.arange(LANES)[None, None, :]).astype(bf16)
    counts = jnp.einsum("ilh,ilr->ihr", left, right, preferred_element_type=f32)
    partial = jnp.dot(
        counts.reshape(every_image, rows_dev), table[0],
        precision=lax.Precision.HIGHEST, preferred_element_type=f32,
    )
    shares = lax.all_to_all(
        partial.reshape(devices, images, proj_width), BOTH, 0, 0, tiled=True
    )
    sums = broadcast_all(jnp.sum(shares, axis=0), devices).reshape(every_image, proj_width)
    counts = jnp.transpose(counts, (1, 0, 2)).astype(bf16)

    padded = -(-seq // 16) * 16
    tokens = jnp.pad(hidden, ((0, 0), (0, padded - seq), (0, 0))).reshape(images * padded, width)
    normed = norm_rows(tokens.astype(f32), ln1_gain).astype(bf16)
    qkv = project_qkv(qkv_w, pos, normed)
    mixed = attend(qkv, images, padded, seq, width)
    resid, normed_two = project_out(out_w, pos, mixed, tokens, ln2_gain)
    active = project_up(up_w, pos, normed_two)
    pooled = project_down(down_w, pos, active, resid, post_gain, images, seq, devices)
    every = lax.all_to_all(pooled, BOTH, 0, 0, tiled=True).reshape(every_image, width)
    table_new, accum_new, content_grad, proj_grad = update(
        pos, every, w_proj, sums, counts, table[0], accum[0], images, width // devices
    )
    return table_new[None], accum_new[None], content_grad, proj_grad


def solution(mesh):
    rows = P(("grp", "fsdp"), None)
    deep = P(("grp", "fsdp"), None, None)
    split = P("fsdp", None)
    placed = (
        deep, P(), split, split, P(), split, split, P(), P(), deep, deep, P(), rows, P(("grp", "fsdp")),
    )
    return jax.shard_map(
        on_device, mesh=mesh, in_specs=placed, out_specs=(deep, deep, rows, rows), check_vma=False
    )
```

```python
import functools
import math

import jax
import jax.numpy as jnp
from jax import lax
from jax.experimental import pallas as pl
from jax.experimental.pallas import tpu as pltpu
from jax.sharding import PartitionSpec as P

HEADS = 16
LOOK_IMG = 64
CORES = 2
LANES = 128
MIB = 1 << 20
ROOM = 58

epsilon = 1e-06
learn_rate = 0.5
bf16 = jnp.bfloat16
f32 = jnp.float32
BOTH = ("grp", "fsdp")

VMEM = pl.BlockSpec(memory_space=pltpu.VMEM)
SMEM = pl.BlockSpec(memory_space=pltpu.SMEM)
ANY = pl.BlockSpec(memory_space=pl.ANY)
SHORT = pl.CostEstimate(flops=1, bytes_accessed=1, transcendentals=0)


def norm_rows(values, gain):
    center = jnp.mean(values, axis=-1, keepdims=True)
    shifted = values - center
    spread = jnp.mean(shifted * shifted, axis=-1, keepdims=True)
    return shifted * lax.rsqrt(spread + epsilon) * gain


def after(values, *others):
    return lax.optimization_barrier((tuple(values), tuple(others)))[0]


class Routes:
    def __init__(self, grp, fsdp):
        self.grp, self.fsdp, self.chips = grp, fsdp, fsdp // CORES

    def moved(self, value, target):
        pairs = []
        for index in range(self.grp * self.fsdp):
            plane, rest = divmod(index, self.fsdp)
            chip, core = divmod(rest, CORES)
            there = target(plane, chip, core)
            pairs.append((index, (there[0] * self.chips + there[1]) * CORES + there[2]))
        return lax.ppermute(value, BOTH, pairs)

    def along(self, value, *steps):
        return [
            self.moved(value, lambda g, c, k, step=step: (g, (c - step) % self.chips, k))
            for step in steps
        ]

    def swap(self, value, bit):
        return self.moved(value, lambda g, c, k: (g ^ bit, c, k))

    def sibling(self, value):
        return self.moved(value, lambda g, c, k: (g, c, k ^ 1))


def quarter_of(shards, plane):
    return jnp.concatenate(
        [
            lax.dynamic_slice_in_dim(s, plane * (s.shape[1] // 4), s.shape[1] // 4, axis=1)
            for s in shards
        ],
        axis=1,
    )


def piece_plan(chips, rows, wide, offset, halved):
    plan = []
    half = (chips - 1) * rows // 2
    for turn in range(3):
        for step in range(1, chips):
            for side in range(2):
                plan.append((1 + turn, (step - 1) * rows, rows, offset, side, step, 0, turn))
    for step in range(1, chips):
        for side in range(2):
            if not halved:
                plan.append((3 + step, 0, rows, offset, side, step, 0, 3))
                continue
            first, last = (step - 1) * rows, step * rows
            for buffer, low, high, base in ((4, 0, half, 0), (5, half, 2 * half, half)):
                start, stop = max(first, low), min(last, high)
                if start < stop:
                    plan.append(
                        (buffer, start - base, stop - start, offset, side, step, start - first, 3)
                    )
    return plan


class Weight:
    def __init__(self, shape, wide, pieces, plan, chips, rows):
        self.shape, self.wide, self.pieces = shape, wide, pieces
        self.plan, self.chips, self.rows = plan, chips, rows

    @property
    def count(self):
        return len(self.pieces)

    @property
    def copies(self):
        return 1 if self.plan is None else 2 + len(self.plan)

    def start(self, refs, whole, sems, pos):
        if self.plan is None:
            copy = pltpu.make_async_copy(refs[0], whole, sems.at[0])
            copy.start()
            return [[copy], [], [], []]
        plane, chip, core = pos[0], pos[1], pos[2]
        groups = [[], [], [], []]
        number, half = 0, self.count // 2

        def go(source, target, turn):
            nonlocal number
            copy = pltpu.make_async_copy(source, target, sems.at[number])
            copy.start()
            groups[turn].append(copy)
            number += 1

        for side in range(2):
            row = pl.multiple_of((chip * CORES + (core ^ side)) * self.rows, self.rows)
            go(refs[side * half], whole.at[pl.ds(row, self.rows), :], 0)
        for buffer, low, count, column, side, step, inner, turn in self.plan:
            there = lax.rem(chip + step, self.chips)
            row = (there * CORES + (core ^ side)) * self.rows + inner
            row = pl.multiple_of(row, math.gcd(self.rows, inner) if inner else self.rows)
            left = pl.multiple_of((plane ^ turn) * self.wide, LANES)
            go(
                refs[side * half + buffer].at[pl.ds(low, count), pl.ds(column, self.wide)],
                whole.at[pl.ds(row, count), pl.ds(left, self.wide)],
                turn,
            )
        return groups

    def each_turn(self, refs, whole, sems, pos, body):
        groups = self.start(refs, whole, sems, pos)
        for turn in range(4):
            for copy in groups[turn]:
                copy.wait()
            left = (pos[0] ^ turn) * self.wide if self.plan is not None else turn * self.wide
            body(left)


def weights_of(shards, pieces, chips, rows, halved):
    found, offset = [], 0
    sent, other, other_own = pieces
    for number, shard in enumerate(shards):
        wide = shard.shape[1] // 4
        found.append(
            Weight(
                (rows * chips * CORES, shard.shape[1]), wide,
                [shard] + sent + [other_own[number]] + other,
                piece_plan(chips, rows, wide, offset, halved), chips, rows,
            )
        )
        offset += wide
    return found


def whole_weight(shard, fsdp):
    full = lax.all_gather(shard, "fsdp", axis=0, tiled=True)
    return Weight(full.shape, shard.shape[1] // 4, [full], None, fsdp // CORES, shard.shape[0])


def block_of(wide):
    return next(size for size in (1024, 768, 512, 256, LANES) if wide % size == 0)


def call_with_weight(weight, body, pos, inputs, out_shapes, scratch, room, name):
    n_in, n_out = len(inputs), len(out_shapes)

    def kernel(*refs):
        pos_ref = refs[0]
        pieces = refs[1 : 1 + weight.count]
        refs = refs[1 + weight.count :]
        ins, outs, rest = refs[:n_in], refs[n_in : n_in + n_out], refs[n_in + n_out :]
        whole, sems = rest[0], rest[1]

        def each_turn(work):
            weight.each_turn(pieces, whole, sems, pos_ref, work)

        body(ins, outs, rest[2:], whole, each_turn)

    return pl.pallas_call(
        kernel,
        out_shape=out_shapes,
        in_specs=[SMEM] + [ANY] * weight.count + [VMEM] * n_in,
        out_specs=[VMEM] * n_out,
        scratch_shapes=[
            pltpu.VMEM(weight.shape, bf16),
            pltpu.SemaphoreType.DMA((weight.copies,)),
        ]
        + list(scratch),
        compiler_params=pltpu.CompilerParams(vmem_limit_bytes=room * MIB),
        cost_estimate=SHORT,
        name=name,
    )(pos, *weight.pieces, *inputs)


def dot32(left, right):
    return jnp.dot(left, right, preferred_element_type=f32)


def column_loop(wide, left, work):
    size = block_of(wide)

    @pl.loop(0, wide // size)
    def _(number):
        work(pl.ds(pl.multiple_of(left + number * size, LANES), size))


def prepare(hidden, gain, padded):
    images, seq, width = hidden.shape
    full = seq // 16

    def kernel(hidden_ref, gain_ref, tokens, normed):
        for image in range(images):
            for number in range(padded // 16):
                at = slice(image * padded + number * 16, image * padded + (number + 1) * 16)
                if number < full:
                    part = hidden_ref[image, number * 16 : (number + 1) * 16, :]
                    tokens[at, :] = part
                    rows = part.astype(f32)
                else:
                    index = lax.broadcasted_iota(jnp.int32, (16, 1), 0)
                    rows = jnp.zeros((16, width), f32)
                    for extra in range(seq - number * 16):
                        row = hidden_ref[image, pl.ds(number * 16 + extra, 1), :].astype(f32)
                        rows = jnp.where(index == extra, row, rows)
                    tokens[at, :] = rows.astype(bf16)
                normed[at, :] = norm_rows(rows, gain_ref[...]).astype(bf16)

    shape = jax.ShapeDtypeStruct((images * padded, width), bf16)
    return pl.pallas_call(
        kernel, out_shape=[shape, shape], in_specs=[VMEM, VMEM], out_specs=[VMEM, VMEM],
        compiler_params=pltpu.CompilerParams(vmem_limit_bytes=16 * MIB),
        cost_estimate=SHORT, name="prepare",
    )(hidden, gain.reshape(1, -1))


def project_qkv(weight, pos, normed):
    def body(ins, outs, scratch, whole, each_turn):
        def quarter(left):
            def work(columns):
                outs[0][:, columns] = dot32(ins[0][...], whole[:, columns]).astype(bf16)

            column_loop(weight.wide, left, work)

        each_turn(quarter)

    rows = normed.shape[0]
    return call_with_weight(
        weight, body, pos, [normed],
        [jax.ShapeDtypeStruct((rows, weight.shape[1]), bf16)], [], ROOM, "project_qkv",
    )[0]


def attend(qkv, seq, width):
    images, padded = qkv.shape[:2]
    head_dim = width // HEADS
    per = LANES // head_dim
    wide = math.gcd(width, 4 * LANES)
    blocks = width // wide
    factor = 1.0 / (math.sqrt(head_dim) * math.log(2.0))

    def kernel(query, keys, values, out):
        lane = lax.broadcasted_iota(jnp.int32, (1, LANES), 1)
        column = lax.broadcasted_iota(jnp.int32, (1, padded), 1)
        for pair in range(wide // LANES):
            at = slice(pair * LANES, (pair + 1) * LANES)
            q, k, v = query[0, :, at], keys[0, :, at], values[0, :, at]
            beside = jnp.concatenate([v, jnp.ones_like(v)], axis=1)
            total = None
            for head in range(per):
                own = (lane // head_dim) == head
                scores = lax.dot_general(
                    jnp.where(own, q, jnp.zeros_like(q)), k,
                    (((1,), (1,)), ((), ())), preferred_element_type=f32,
                )
                scores = jnp.where(column < seq, scores, -1e30)
                top = jnp.max(scores, axis=-1, keepdims=True)
                probs = jnp.exp2((scores - top) * factor).astype(bf16)
                both = dot32(probs, beside)
                mixed = both[:, :LANES] / both[:, LANES:]
                total = mixed if total is None else jnp.where(own, mixed, total)
            out[0, :, at] = total.astype(bf16)

    spec = lambda shift: pl.BlockSpec((1, padded, wide), lambda i, h: (i, 0, h + shift * blocks))
    return pl.pallas_call(
        kernel,
        grid=(images, blocks),
        out_shape=jax.ShapeDtypeStruct((images, padded, width), bf16),
        in_specs=[spec(0), spec(1), spec(2)],
        out_specs=spec(0),
        compiler_params=pltpu.CompilerParams(vmem_limit_bytes=ROOM * MIB),
        cost_estimate=SHORT,
        name="attend",
    )(qkv, qkv, qkv)


def project_out(weight, pos, mixed, tokens, gain):
    rows, width = mixed.shape

    def body(ins, outs, scratch, whole, each_turn):
        mixed_ref, tokens_ref, gain_ref = ins
        resid, normed = outs

        def quarter(left):
            def work(columns):
                product = dot32(mixed_ref[...], whole[:, columns])
                resid[:, columns] = (tokens_ref[:, columns].astype(f32) + product).astype(bf16)

            column_loop(weight.wide, left, work)

        each_turn(quarter)
        for number in range(rows // 16):
            at = slice(number * 16, (number + 1) * 16)
            normed[at, :] = norm_rows(resid[at, :].astype(f32), gain_ref[...]).astype(bf16)

    shape = jax.ShapeDtypeStruct((rows, width), bf16)
    return call_with_weight(
        weight, body, pos, [mixed, tokens, gain.reshape(1, -1)], [shape, shape], [], ROOM, "project_out",
    )


def gelu(values):
    return 0.5 * values * (1.0 + lax.erf(values * math.sqrt(0.5)))


def project_up(weight, pos, normed):
    rows = normed.shape[0]

    def body(ins, outs, scratch, whole, each_turn):
        def quarter(left):
            def work(columns):
                outs[0][:, columns] = gelu(dot32(ins[0][...], whole[:, columns])).astype(bf16)

            column_loop(weight.wide, left, work)

        each_turn(quarter)

    return call_with_weight(
        weight, body, pos, [normed],
        [jax.ShapeDtypeStruct((rows, weight.shape[1]), bf16)], [], ROOM, "project_up",
    )[0]


def thirds(values):
    first = values.astype(bf16)
    left = values - first.astype(f32)
    second = left.astype(bf16)
    return first, second, (left - second.astype(f32)).astype(bf16)


def project_down(weight, pos, active, resid, gain, sums, images, seq, devices):
    rows, width = resid.shape
    padded = rows // images

    def body(ins, outs, scratch, whole, each_turn):
        active_ref, resid_ref, gain_ref, sums_ref = ins
        (final,) = scratch
        (pooled,) = outs
        split = [part.astype(f32) for part in thirds(sums_ref[...])]

        def quarter(left):
            def work(columns):
                product = dot32(active_ref[...], whole[:, columns])
                final[:, columns] = resid_ref[:, columns].astype(f32) + product

            column_loop(weight.wide, left, work)

        each_turn(quarter)
        step = 16
        for image in range(images):
            total = jnp.zeros((step, width), f32)
            for number in range(padded // step):
                at = slice(image * padded + number * step, image * padded + (number + 1) * step)
                posted = norm_rows(final[at, :], gain_ref[...])
                if (number + 1) * step > seq:
                    row = lax.broadcasted_iota(jnp.int32, (step, 1), 0) + number * step
                    posted = jnp.where(row < seq, posted, 0.0)
                total = total + posted
            mean = jnp.sum(total, axis=0, keepdims=True) / seq
            at = slice(image, image + 1)
            row = jnp.concatenate([mean] + [part[at, :] for part in split], axis=1).astype(bf16)
            for device in range(devices):
                pooled[device, at, :] = row

    return call_with_weight(
        weight, body, pos, [active, resid, gain.reshape(1, -1), sums],
        [jax.ShapeDtypeStruct((devices, images, width + 3 * sums.shape[1]), bf16)],
        [pltpu.VMEM((rows, width), f32)], ROOM, "project_down",
    )[0]


def update(pos, every, proj, named, table, accum, images, share):
    rows, width = table.shape
    every_image, depth = every.shape[0], proj.shape[0]
    blocks = rows // LANES
    per = 4 if blocks % 4 == 0 else 1
    side = max(share, LANES)
    over = (((0,), (0,)), ((), ()))

    def kernel(pos_ref, every_ref, proj_ref, named_ref, table_ref, accum_ref,
               table_out, accum_out, content_out, proj_out, units, grads, square):
        @pl.when(pl.program_id(0) == 0)
        def _():
            content = dot32(every_ref[:, :depth], proj_ref[...])
            scale = lax.rsqrt(jnp.mean(content * content, axis=-1, keepdims=True) + epsilon)
            unit = content * scale
            for number, part in enumerate(thirds(unit)):
                units[:, number * width : (number + 1) * width] = part
            units[:, 3 * width :] = jnp.ones((every_image, width), bf16)
            sums = sum(
                every_ref[:, depth + part * width : depth + (part + 1) * width].astype(f32)
                for part in range(3)
            )
            grad_unit = LOOK_IMG * unit - sums
            inner = jnp.mean(grad_unit * unit, axis=-1, keepdims=True)
            grad = scale * (grad_unit - unit * inner)
            grads[...] = grad
            me = pos_ref[3]
            for image in range(images):
                content_out[image : image + 1, :] = grads[pl.ds(me * images + image, 1), :]
            column = me * share
            block = pl.multiple_of((column // side) * side, side)
            mine = every_ref[:, pl.ds(block, side)]
            total = None
            for part in thirds(grad):
                product = lax.dot_general(mine, part, over, preferred_element_type=f32)
                total = product if total is None else total + product
            square[...] = total
            unit_rows = math.gcd(share, side)
            proj_out[...] = square[pl.ds(pl.multiple_of(column - block, unit_rows), share), :]

        for number in range(per):
            at = slice(number * LANES, (number + 1) * LANES)
            found = dot32(named_ref[at, :], units[...])
            taken = found[:, :width] + found[:, width : 2 * width] + found[:, 2 * width : 3 * width]
            old = table_ref[at, :]
            grad_rows = found[:, 3 * width :] * old - taken
            grown = accum_ref[at, :] + grad_rows * grad_rows
            accum_out[at, :] = grown
            table_out[at, :] = old - learn_rate * grad_rows / jnp.sqrt(grown)

    whole = lambda shape: pl.BlockSpec(shape, lambda i: (0,) * len(shape))
    strip = pl.BlockSpec((per * LANES, width), lambda i: (i, 0))
    return pl.pallas_call(
        kernel,
        grid=(blocks // per,),
        out_shape=[
            jax.ShapeDtypeStruct(table.shape, f32),
            jax.ShapeDtypeStruct(table.shape, f32),
            jax.ShapeDtypeStruct((images, width), f32),
            jax.ShapeDtypeStruct((share, width), f32),
        ],
        in_specs=[
            SMEM, whole(every.shape), whole(proj.shape),
            pl.BlockSpec((per * LANES, every_image), lambda i: (i, 0)), strip, strip,
        ],
        out_specs=[strip, strip, whole((images, width)), whole((share, width))],
        scratch_shapes=[
            pltpu.VMEM((every_image, 4 * width), bf16),
            pltpu.VMEM((every_image, width), f32),
            pltpu.VMEM((side, width), f32),
        ],
        compiler_params=pltpu.CompilerParams(vmem_limit_bytes=ROOM * MIB),
        name="update",
    )(pos, every, proj, named, table, accum)


def broadcast_all(value, devices):
    return lax.all_to_all(
        jnp.broadcast_to(value[None], (devices,) + value.shape), BOTH, 0, 0, tiled=True
    )


def count_rows(named, table, mine, images):
    rows_dev = table.shape[0]
    tables = named[:, 0].reshape(images, LOOK_IMG)
    spots = named[:, 1].reshape(images, LOOK_IMG)
    high = jnp.where(tables == mine, spots // LANES, -1)
    left = (high[:, :, None] == jnp.arange(rows_dev // LANES)[None, None, :]).astype(bf16)
    right = ((spots % LANES)[:, :, None] == jnp.arange(LANES)[None, None, :]).astype(bf16)
    counts = jnp.einsum("ilh,ilr->ihr", left, right, preferred_element_type=f32)
    partial = jnp.dot(
        counts.reshape(images, rows_dev), table,
        precision=lax.Precision.HIGHEST, preferred_element_type=f32,
    )
    return jnp.transpose(counts, (1, 2, 0)).reshape(rows_dev, images).astype(bf16), partial


def on_device(
    hidden, ln1_gain, w_qkv, w_out, ln2_gain, w_up, w_down, post_gain, w_proj,
    table, accum, place, lookup_table, lookup_row,
):
    images, seq, width = hidden.shape
    grp, fsdp = lax.axis_size("grp"), lax.axis_size("fsdp")
    devices = grp * fsdp
    plane, spot = lax.axis_index("grp"), lax.axis_index("fsdp")
    me = plane * fsdp + spot
    pos = jnp.stack([plane, spot // CORES, spot % CORES, me]).astype(jnp.int32)

    rows = w_qkv.shape[0]
    routes = Routes(grp, fsdp)
    chips = routes.chips
    simple = grp == 4 and fsdp % CORES == 0 and chips % 2 == 0 and rows % LANES == 0
    joined = lambda parts: jnp.concatenate(parts, axis=0)
    half = (chips - 1) * rows // 2
    middle = chips // 2
    near = [step for step in range(1, chips) if step != middle]
    padded = -(-seq // 16) * 16
    tokens, normed = prepare(hidden, ln1_gain, padded)
    if simple:
        first = quarter_of([w_qkv, w_out], plane)
        a_one = joined(routes.along(first, *range(1, chips)))
        own = [routes.sibling(w) for w in after([w_qkv, w_out], first)]
        own += [routes.sibling(w) for w in after([w_up, w_down], own, normed)]
        second, third, fourth = (
            quarter_of([w_up], plane), quarter_of([w_down], plane), quarter_of([w_down], plane ^ 3),
        )

    rows_dev, proj_width = table.shape[1:]
    every_image = images * devices
    my_table = jnp.sum(jnp.where(place == me, jnp.arange(place.shape[0], dtype=jnp.int32), 0))
    named = broadcast_all(jnp.stack([lookup_table[:, 0], lookup_row]), devices)
    per_device = lambda v: v.reshape(devices, images, proj_width)
    counting = functools.partial(count_rows, table=table[0], mine=my_table, images=every_image)

    if simple:
        a_one, second, third, fourth, named = after([a_one, second, third, fourth, named], own, normed)
        x_one, y_one = routes.swap(a_one, 1), routes.swap(a_one, 2)
        ends = routes.along(second, *near)
        a_one_other = routes.sibling(a_one)
        counts, partial = counting(named)
        x_one, y_one, second, counts, partial = after(
            [x_one, y_one, second, counts, partial], ends, a_one_other
        )
        low_one, high_one = routes.swap(x_one[:half], 2), routes.swap(y_one[half:], 1)
        mid = routes.along(second, middle)
        a_two = joined(ends[: middle - 1] + mid + ends[middle - 1 :])
        other = [a_one_other] + [routes.sibling(v) for v in (x_one, y_one)]
        low_one, high_one, a_two, third = after(
            [low_one, high_one, a_two, third], other
        )
        other = other + [routes.sibling(v) for v in (low_one, high_one)]
        pieces = [a_one, x_one, y_one, low_one, high_one], other, own[:2]
        qkv_w, out_w = weights_of([w_qkv, w_out], pieces, chips, rows, True)
        x_two, y_two = routes.swap(a_two, 1), routes.swap(a_two, 2)
        ends = routes.along(third, *near)
        (a_two_sent,) = after([a_two], other)
        a_two_other = routes.sibling(a_two_sent)
        qkv = project_qkv(qkv_w, pos, normed)
        mixed = attend(qkv.reshape(images, padded, 3 * width), seq, width)
        x_two, y_two, ends, mixed, third, a_two_other = after(
            [x_two, y_two, ends, mixed, third, a_two_other]
        )
        mixed = mixed.reshape(images * padded, width)
        low_two, high_two = routes.swap(x_two[:half], 2), routes.swap(y_two[half:], 1)
        mid = routes.along(third, middle)
        other = [a_two_other] + [routes.sibling(v) for v in (x_two, y_two)]
        resid, normed_two = project_out(out_w, pos, mixed, tokens, ln2_gain)
        low_two, high_two, mid, other, normed_two = after([low_two, high_two, mid, other, normed_two])
        other = other + [routes.sibling(v) for v in (low_two, high_two)]
        pieces = [a_two, x_two, y_two, low_two, high_two], other, own[2:3]
        (up_w,) = weights_of([w_up], pieces, chips, rows, True)
        a_three = joined(ends[: middle - 1] + mid + ends[middle - 1 :])
        x_three, y_three = routes.swap(a_three, 1), routes.swap(a_three, 2)
        ends = routes.along(fourth, *near)
        (normed_two,) = after([normed_two], other)
        active = project_up(up_w, pos, normed_two)
        active, partial, a_three_sent, x_three, y_three, ends, fourth = after(
            [active, partial, a_three, x_three, y_three, ends, fourth]
        )
        mid = routes.along(fourth, middle)
        other = [routes.sibling(v) for v in (a_three_sent, x_three, y_three)]
        sums = jnp.sum(lax.all_to_all(per_device(partial), BOTH, 0, 0, tiled=True), axis=0)
        ends, mid, other = after([ends, mid, other], sums)
        diagonal = ends[: middle - 1] + mid + ends[middle - 1 :]
        other = other + [routes.sibling(v) for v in diagonal]
        pieces = [a_three, x_three, y_three] + diagonal, other, own[3:]
        (down_w,) = weights_of([w_down], pieces, chips, w_down.shape[0], False)
    else:
        counts, partial = counting(named)
        sums = jnp.sum(lax.all_to_all(per_device(partial), BOTH, 0, 0, tiled=True), axis=0)
        qkv_w, out_w, up_w, down_w = [whole_weight(w, fsdp) for w in (w_qkv, w_out, w_up, w_down)]
        qkv = project_qkv(qkv_w, pos, normed).reshape(images, padded, 3 * width)
        mixed = attend(qkv, seq, width).reshape(images * padded, width)
        resid, normed_two = project_out(out_w, pos, mixed, tokens, ln2_gain)
        active = project_up(up_w, pos, normed_two)
    pooled = project_down(down_w, pos, active, resid, post_gain, sums, images, seq, devices)
    every = lax.all_to_all(pooled, BOTH, 0, 0, tiled=True).reshape(every_image, -1)
    table_new, accum_new, content_grad, proj_grad = update(
        pos, every, w_proj, counts, table[0], accum[0], images, width // devices
    )
    return table_new[None], accum_new[None], content_grad, proj_grad


def solution(mesh):
    rows = P(("grp", "fsdp"), None)
    deep = P(("grp", "fsdp"), None, None)
    split = P("fsdp", None)
    placed = (
        deep, P(), split, split, P(), split, split, P(), P(), deep, deep, P(), rows, P(("grp", "fsdp")),
    )
    return jax.shard_map(
        on_device, mesh=mesh, in_specs=placed, out_specs=(deep, deep, rows, rows), check_vma=False
    )
```

```python
import functools
import math

import jax
import jax.numpy as jnp
from jax import lax
from jax.experimental import pallas as pl
from jax.experimental.pallas import tpu as pltpu
from jax.sharding import PartitionSpec as P

HEADS = 16
LOOK_IMG = 64
CORES = 2
LANES = 128
MIB = 1 << 20
ROOM = 58

epsilon = 1e-06
learn_rate = 0.5
bf16 = jnp.bfloat16
f32 = jnp.float32
BOTH = ("grp", "fsdp")

VMEM = pl.BlockSpec(memory_space=pltpu.VMEM)
SMEM = pl.BlockSpec(memory_space=pltpu.SMEM)
ANY = pl.BlockSpec(memory_space=pl.ANY)
SHORT = pl.CostEstimate(flops=1, bytes_accessed=1, transcendentals=0)


def norm_rows(values, gain):
    center = jnp.mean(values, axis=-1, keepdims=True)
    shifted = values - center
    spread = jnp.mean(shifted * shifted, axis=-1, keepdims=True)
    return shifted * lax.rsqrt(spread + epsilon) * gain


def after(values, *others):
    return lax.optimization_barrier((tuple(values), tuple(others)))[0]


class Routes:
    def __init__(self, grp, fsdp):
        self.grp, self.fsdp, self.chips = grp, fsdp, fsdp // CORES

    def moved(self, value, target):
        pairs = []
        for index in range(self.grp * self.fsdp):
            plane, rest = divmod(index, self.fsdp)
            chip, core = divmod(rest, CORES)
            there = target(plane, chip, core)
            pairs.append((index, (there[0] * self.chips + there[1]) * CORES + there[2]))
        return lax.ppermute(value, BOTH, pairs)

    def along(self, value, *steps):
        return [
            self.moved(value, lambda g, c, k, step=step: (g, (c - step) % self.chips, k))
            for step in steps
        ]

    def swap(self, value, bit):
        return self.moved(value, lambda g, c, k: (g ^ bit, c, k))

    def sibling(self, value):
        return self.moved(value, lambda g, c, k: (g, c, k ^ 1))


def quarter_of(shards, plane):
    return jnp.concatenate(
        [
            lax.dynamic_slice_in_dim(s, plane * (s.shape[1] // 4), s.shape[1] // 4, axis=1)
            for s in shards
        ],
        axis=1,
    )


def piece_plan(chips, rows, wide, offset, halved):
    plan = []
    half = (chips - 1) * rows // 2
    for turn in range(3):
        for step in range(1, chips):
            for side in range(2):
                plan.append((1 + turn, (step - 1) * rows, rows, offset, side, step, 0, turn))
    for step in range(1, chips):
        for side in range(2):
            if not halved:
                plan.append((3 + step, 0, rows, offset, side, step, 0, 3))
                continue
            first, last = (step - 1) * rows, step * rows
            for buffer, low, high, base in ((4, 0, half, 0), (5, half, 2 * half, half)):
                start, stop = max(first, low), min(last, high)
                if start < stop:
                    plan.append(
                        (buffer, start - base, stop - start, offset, side, step, start - first, 3)
                    )
    return plan


class Weight:
    def __init__(self, shape, wide, pieces, plan, chips, rows):
        self.shape, self.wide, self.pieces = shape, wide, pieces
        self.plan, self.chips, self.rows = plan, chips, rows

    @property
    def count(self):
        return len(self.pieces)

    @property
    def copies(self):
        return 4 if self.plan is None else 8 + len(self.plan)

    def quarter(self, pos, turn):
        return turn if self.plan is None else pos[0] ^ turn

    def moves(self, refs, whole, sems, pos):
        groups = [[], [], [], []]
        number, half = 0, self.count // 2

        def go(source, target, turn):
            nonlocal number
            groups[turn].append(pltpu.make_async_copy(source, target, sems.at[number]))
            number += 1

        for turn in range(4):
            columns = pl.ds(pl.multiple_of(self.quarter(pos, turn) * self.wide, LANES), self.wide)
            if self.plan is None:
                go(refs[0].at[:, columns], whole.at[turn], turn)
                continue
            chip, core = pos[1], pos[2]
            for side in range(2):
                row = pl.multiple_of((chip * CORES + (core ^ side)) * self.rows, self.rows)
                go(refs[side * half].at[:, columns], whole.at[turn, pl.ds(row, self.rows), :], turn)
            for buffer, low, count, column, side, step, inner, own in self.plan:
                if own != turn:
                    continue
                there = lax.rem(chip + step, self.chips)
                row = (there * CORES + (core ^ side)) * self.rows + inner
                row = pl.multiple_of(row, math.gcd(self.rows, inner) if inner else self.rows)
                go(
                    refs[side * half + buffer].at[pl.ds(low, count), pl.ds(column, self.wide)],
                    whole.at[turn, pl.ds(row, count), :],
                    turn,
                )
        return groups


def weights_of(shards, pieces, chips, rows, halved):
    found, offset = [], 0
    sent, other, other_own = pieces
    for number, shard in enumerate(shards):
        wide = shard.shape[1] // 4
        found.append(
            Weight(
                (rows * chips * CORES, shard.shape[1]), wide,
                [shard] + sent + [other_own[number]] + other,
                piece_plan(chips, rows, wide, offset, halved), chips, rows,
            )
        )
        offset += wide
    return found


def whole_weight(shard, fsdp):
    full = lax.all_gather(shard, "fsdp", axis=0, tiled=True)
    return Weight(full.shape, shard.shape[1] // 4, [full], None, fsdp // CORES, shard.shape[0])


def call_with_weight(weight, body, pos, inputs, outs, scratch, room, name):
    n_in, n_out = len(inputs), len(outs)

    def kernel(*refs):
        pos_ref, refs = refs[0], refs[1:]
        pieces, refs = refs[: weight.count], refs[weight.count :]
        sources, refs = refs[:n_in], refs[n_in:]
        targets, refs = refs[:n_out], refs[n_out:]
        whole, sems, in_sems, out_sem = refs[:4]
        ins, refs = refs[4 : 4 + n_in], refs[4 + n_in :]
        held, rest = refs[:n_out], refs[n_out:]
        first = [
            pltpu.make_async_copy(source, target, in_sems.at[number])
            for number, (source, target) in enumerate(zip(sources, ins, strict=True))
        ]
        for copy in first:
            copy.start()
        groups = weight.moves(pieces, whole, sems, pos_ref)
        for copy in groups[0]:
            copy.start()
        sent = []

        def each_turn(work):
            for copy in first:
                copy.wait()
            for turn in range(4):
                for copy in groups[turn]:
                    copy.wait()
                for copy in groups[turn + 1] if turn < 3 else []:
                    copy.start()
                left = pl.multiple_of(weight.quarter(pos_ref, turn) * weight.wide, LANES)
                work(turn, whole.at[turn], pl.ds(left, weight.wide))

        def flush(number, *at):
            copy = pltpu.make_async_copy(
                held[number].at[at], targets[number].at[at], out_sem.at[len(sent)]
            )
            copy.start()
            sent.append(copy)

        body(ins, held, rest, each_turn, flush)
        for copy in sent:
            copy.wait()

    return pl.pallas_call(
        kernel,
        out_shape=outs,
        in_specs=[SMEM] + [ANY] * (weight.count + n_in),
        out_specs=[ANY] * n_out,
        scratch_shapes=[
            pltpu.VMEM((4, weight.shape[0], weight.wide), bf16),
            pltpu.SemaphoreType.DMA((weight.copies,)),
            pltpu.SemaphoreType.DMA((n_in,)),
            pltpu.SemaphoreType.DMA((8,)),
        ]
        + [pltpu.VMEM(v.shape, v.dtype) for v in inputs]
        + [pltpu.VMEM(v.shape, v.dtype) for v in outs]
        + list(scratch),
        compiler_params=pltpu.CompilerParams(vmem_limit_bytes=room * MIB),
        cost_estimate=SHORT,
        name=name,
    )(pos, *weight.pieces, *inputs)


def dot32(left, right):
    return jnp.dot(left, right, preferred_element_type=f32)


def prepare(hidden, gain, padded):
    images, seq, width = hidden.shape
    full = seq // 16

    def kernel(hidden_ref, gain_ref, tokens, normed):
        for image in range(images):
            for number in range(padded // 16):
                at = slice(image * padded + number * 16, image * padded + (number + 1) * 16)
                if number < full:
                    part = hidden_ref[image, number * 16 : (number + 1) * 16, :]
                    tokens[at, :] = part
                    rows = part.astype(f32)
                else:
                    index = lax.broadcasted_iota(jnp.int32, (16, 1), 0)
                    rows = jnp.zeros((16, width), f32)
                    for extra in range(seq - number * 16):
                        row = hidden_ref[image, pl.ds(number * 16 + extra, 1), :].astype(f32)
                        rows = jnp.where(index == extra, row, rows)
                    tokens[at, :] = rows.astype(bf16)
                normed[at, :] = norm_rows(rows, gain_ref[...]).astype(bf16)

    shape = jax.ShapeDtypeStruct((images * padded, width), bf16)
    return pl.pallas_call(
        kernel, out_shape=[shape, shape], in_specs=[VMEM, VMEM], out_specs=[VMEM, VMEM],
        compiler_params=pltpu.CompilerParams(vmem_limit_bytes=16 * MIB),
        cost_estimate=SHORT, name="prepare",
    )(hidden, gain.reshape(1, -1))


def project_qkv(weight, pos, normed):
    def body(ins, outs, scratch, each_turn, flush):
        def quarter(turn, part, columns):
            outs[0][:, columns] = dot32(ins[0][...], part[...]).astype(bf16)
            flush(0, slice(None), columns)

        each_turn(quarter)

    out = jax.ShapeDtypeStruct((normed.shape[0], weight.shape[1]), bf16)
    return call_with_weight(weight, body, pos, [normed], [out], [], ROOM, "project_qkv")[0]


def attend(qkv, seq, width):
    images, padded = qkv.shape[:2]
    head_dim = width // HEADS
    per = LANES // head_dim
    wide = math.gcd(width, 4 * LANES)
    blocks = width // wide
    factor = 1.0 / (math.sqrt(head_dim) * math.log(2.0))

    def kernel(query, keys, values, out):
        lane = lax.broadcasted_iota(jnp.int32, (1, LANES), 1)
        column = lax.broadcasted_iota(jnp.int32, (1, padded), 1)
        for pair in range(wide // LANES):
            at = slice(pair * LANES, (pair + 1) * LANES)
            q, k, v = query[0, :, at], keys[0, :, at], values[0, :, at]
            beside = jnp.concatenate([v, jnp.ones_like(v)], axis=1)
            total = None
            for head in range(per):
                own = (lane // head_dim) == head
                scores = lax.dot_general(
                    jnp.where(own, q, jnp.zeros_like(q)), k,
                    (((1,), (1,)), ((), ())), preferred_element_type=f32,
                )
                scores = jnp.where(column < seq, scores, -1e30)
                top = jnp.max(scores, axis=-1, keepdims=True)
                probs = jnp.exp2((scores - top) * factor).astype(bf16)
                both = dot32(probs, beside)
                mixed = both[:, :LANES] / both[:, LANES:]
                total = mixed if total is None else jnp.where(own, mixed, total)
            out[0, :, at] = total.astype(bf16)

    spec = lambda shift: pl.BlockSpec((1, padded, wide), lambda i, h: (i, 0, h + shift * blocks))
    return pl.pallas_call(
        kernel,
        grid=(images, blocks),
        out_shape=jax.ShapeDtypeStruct((images, padded, width), bf16),
        in_specs=[spec(0), spec(1), spec(2)],
        out_specs=spec(0),
        compiler_params=pltpu.CompilerParams(vmem_limit_bytes=16 * MIB),
        cost_estimate=SHORT,
        name="attend",
    )(qkv, qkv, qkv)


def project_out(weight, pos, mixed, tokens, gain):
    rows, width = mixed.shape

    def body(ins, outs, scratch, each_turn, flush):
        mixed_ref, tokens_ref, gain_ref = ins
        resid, normed = outs

        def quarter(turn, part, columns):
            product = dot32(mixed_ref[...], part[...])
            resid[:, columns] = (tokens_ref[:, columns].astype(f32) + product).astype(bf16)

        each_turn(quarter)
        flush(0, slice(None), slice(None))
        for number in range(rows // 16):
            at = slice(number * 16, (number + 1) * 16)
            normed[at, :] = norm_rows(resid[at, :].astype(f32), gain_ref[...]).astype(bf16)
        flush(1, slice(None), slice(None))

    shape = jax.ShapeDtypeStruct((rows, width), bf16)
    return call_with_weight(
        weight, body, pos, [mixed, tokens, gain.reshape(1, -1)], [shape, shape], [], 12, "project_out"
    )


def gelu(values):
    return 0.5 * values * (1.0 + lax.erf(values * math.sqrt(0.5)))


def project_up(weight, pos, normed):
    size = math.gcd(weight.wide, 512)

    def body(ins, outs, scratch, each_turn, flush):
        def quarter(turn, part, columns):
            for number in range(weight.wide // size):
                left = pl.multiple_of(columns.start + number * size, LANES)
                upward = dot32(ins[0][...], part[:, number * size : (number + 1) * size])
                outs[0][:, pl.ds(left, size)] = gelu(upward).astype(bf16)
            flush(0, slice(None), columns)

        each_turn(quarter)

    out = jax.ShapeDtypeStruct((normed.shape[0], weight.shape[1]), bf16)
    return call_with_weight(weight, body, pos, [normed], [out], [], 20, "project_up")[0]


def thirds(values):
    first = values.astype(bf16)
    left = values - first.astype(f32)
    second = left.astype(bf16)
    return first, second, (left - second.astype(f32)).astype(bf16)


def project_down(weight, pos, active, resid, gain, sums, images, seq, devices):
    rows, width = resid.shape
    padded = rows // images

    def body(ins, outs, scratch, each_turn, flush):
        active_ref, resid_ref, gain_ref, sums_ref = ins
        (final,) = scratch
        (pooled,) = outs

        def quarter(turn, part, columns):
            product = dot32(active_ref[...], part[...])
            final[:, columns] = resid_ref[:, columns].astype(f32) + product

        each_turn(quarter)
        split = [part.astype(f32) for part in thirds(sums_ref[...])]
        step = 16
        for image in range(images):
            total = jnp.zeros((step, width), f32)
            for number in range(padded // step):
                at = slice(image * padded + number * step, image * padded + (number + 1) * step)
                posted = norm_rows(final[at, :], gain_ref[...])
                if (number + 1) * step > seq:
                    row = lax.broadcasted_iota(jnp.int32, (step, 1), 0) + number * step
                    posted = jnp.where(row < seq, posted, 0.0)
                total = total + posted
            mean = jnp.sum(total, axis=0, keepdims=True) / seq
            at = slice(image, image + 1)
            row = jnp.concatenate([mean] + [part[at, :] for part in split], axis=1).astype(bf16)
            for device in range(devices):
                pooled[device, at, :] = row
        flush(0, slice(None), slice(None), slice(None))

    return call_with_weight(
        weight, body, pos, [active, resid, gain.reshape(1, -1), sums],
        [jax.ShapeDtypeStruct((devices, images, width + 3 * sums.shape[1]), bf16)],
        [pltpu.VMEM((rows, width), f32)], 26, "project_down",
    )[0]


def update(pos, every, proj, named, table, accum, images, share):
    rows, width = table.shape
    every_image, depth = every.shape[0], proj.shape[0]
    blocks = rows // LANES
    per = 4 if blocks % 4 == 0 else 1
    side = max(share, LANES)
    over = (((0,), (0,)), ((), ()))

    def kernel(pos_ref, every_ref, proj_ref, named_ref, table_ref, accum_ref,
               table_out, accum_out, content_out, proj_out, units, grads, square):
        @pl.when(pl.program_id(0) == 0)
        def _():
            content = dot32(every_ref[:, :depth], proj_ref[...])
            scale = lax.rsqrt(jnp.mean(content * content, axis=-1, keepdims=True) + epsilon)
            unit = content * scale
            for number, part in enumerate(thirds(unit)):
                units[:, number * width : (number + 1) * width] = part
            units[:, 3 * width :] = jnp.ones((every_image, width), bf16)
            sums = sum(
                every_ref[:, depth + part * width : depth + (part + 1) * width].astype(f32)
                for part in range(3)
            )
            grad_unit = LOOK_IMG * unit - sums
            inner = jnp.mean(grad_unit * unit, axis=-1, keepdims=True)
            grad = scale * (grad_unit - unit * inner)
            grads[...] = grad
            me = pos_ref[3]
            for image in range(images):
                content_out[image : image + 1, :] = grads[pl.ds(me * images + image, 1), :]
            column = me * share
            block = pl.multiple_of((column // side) * side, side)
            mine = every_ref[:, pl.ds(block, side)]
            total = None
            for part in thirds(grad):
                product = lax.dot_general(mine, part, over, preferred_element_type=f32)
                total = product if total is None else total + product
            square[...] = total
            unit_rows = math.gcd(share, side)
            proj_out[...] = square[pl.ds(pl.multiple_of(column - block, unit_rows), share), :]

        for number in range(per):
            at = slice(number * LANES, (number + 1) * LANES)
            found = dot32(named_ref[at, :], units[...])
            taken = found[:, :width] + found[:, width : 2 * width] + found[:, 2 * width : 3 * width]
            old = table_ref[at, :]
            grad_rows = found[:, 3 * width :] * old - taken
            grown = accum_ref[at, :] + grad_rows * grad_rows
            accum_out[at, :] = grown
            table_out[at, :] = old - learn_rate * grad_rows / jnp.sqrt(grown)

    whole = lambda shape: pl.BlockSpec(shape, lambda i: (0,) * len(shape))
    strip = pl.BlockSpec((per * LANES, width), lambda i: (i, 0))
    return pl.pallas_call(
        kernel,
        grid=(blocks // per,),
        out_shape=[
            jax.ShapeDtypeStruct(table.shape, f32),
            jax.ShapeDtypeStruct(table.shape, f32),
            jax.ShapeDtypeStruct((images, width), f32),
            jax.ShapeDtypeStruct((share, width), f32),
        ],
        in_specs=[
            SMEM, whole(every.shape), whole(proj.shape),
            pl.BlockSpec((per * LANES, every_image), lambda i: (i, 0)), strip, strip,
        ],
        out_specs=[strip, strip, whole((images, width)), whole((share, width))],
        scratch_shapes=[
            pltpu.VMEM((every_image, 4 * width), bf16),
            pltpu.VMEM((every_image, width), f32),
            pltpu.VMEM((side, width), f32),
        ],
        compiler_params=pltpu.CompilerParams(vmem_limit_bytes=ROOM * MIB),
        name="update",
    )(pos, every, proj, named, table, accum)


def broadcast_all(value, devices):
    return lax.all_to_all(
        jnp.broadcast_to(value[None], (devices,) + value.shape), BOTH, 0, 0, tiled=True
    )


def count_rows(named, table, mine, images):
    rows_dev = table.shape[0]
    tables = named[:, 0].reshape(images, LOOK_IMG)
    spots = named[:, 1].reshape(images, LOOK_IMG)
    high = jnp.where(tables == mine, spots // LANES, -1)
    left = (high[:, :, None] == jnp.arange(rows_dev // LANES)[None, None, :]).astype(bf16)
    right = ((spots % LANES)[:, :, None] == jnp.arange(LANES)[None, None, :]).astype(bf16)
    counts = jnp.einsum("ilh,ilr->ihr", left, right, preferred_element_type=f32)
    partial = jnp.dot(
        counts.reshape(images, rows_dev), table,
        precision=lax.Precision.HIGHEST, preferred_element_type=f32,
    )
    return jnp.transpose(counts, (1, 2, 0)).reshape(rows_dev, images).astype(bf16), partial


def on_device(
    hidden, ln1_gain, w_qkv, w_out, ln2_gain, w_up, w_down, post_gain, w_proj,
    table, accum, place, lookup_table, lookup_row,
):
    images, seq, width = hidden.shape
    grp, fsdp = lax.axis_size("grp"), lax.axis_size("fsdp")
    devices = grp * fsdp
    plane, spot = lax.axis_index("grp"), lax.axis_index("fsdp")
    me = plane * fsdp + spot
    pos = jnp.stack([plane, spot // CORES, spot % CORES, me]).astype(jnp.int32)

    rows = w_qkv.shape[0]
    routes = Routes(grp, fsdp)
    chips = routes.chips
    simple = grp == 4 and fsdp % CORES == 0 and chips % 2 == 0 and rows % LANES == 0
    joined = lambda parts: jnp.concatenate(parts, axis=0)
    half = (chips - 1) * rows // 2
    middle = chips // 2
    near = [step for step in range(1, chips) if step != middle]
    padded = -(-seq // 16) * 16
    tokens, normed = prepare(hidden, ln1_gain, padded)
    if simple:
        first = quarter_of([w_qkv, w_out], plane)
        ends = routes.along(first, *near)
        mid = routes.along(first, middle)
        own = [routes.sibling(w) for w in after([w_qkv, w_out], first)]
        a_one = joined(ends[: middle - 1] + mid + ends[middle - 1 :])
        second, third, fourth = (
            quarter_of([w_up], plane), quarter_of([w_down], plane), quarter_of([w_down], plane ^ 3),
        )

    rows_dev, proj_width = table.shape[1:]
    every_image = images * devices
    my_table = jnp.sum(jnp.where(place == me, jnp.arange(place.shape[0], dtype=jnp.int32), 0))
    named = broadcast_all(jnp.stack([lookup_table[:, 0], lookup_row]), devices)
    per_device = lambda v: v.reshape(devices, images, proj_width)
    counting = functools.partial(count_rows, table=table[0], mine=my_table, images=every_image)

    if simple:
        a_one, second, third, fourth, named = after([a_one, second, third, fourth, named], own, normed)
        x_one, y_one = routes.swap(a_one, 1), routes.swap(a_one, 2)
        ends = routes.along(second, *near)
        a_one_other = routes.sibling(a_one)
        counts, partial = counting(named)
        x_one, y_one, second, counts, partial = after(
            [x_one, y_one, second, counts, partial], ends, a_one_other
        )
        low_one, high_one = routes.swap(x_one[:half], 2), routes.swap(y_one[half:], 1)
        mid = routes.along(second, middle)
        a_two = joined(ends[: middle - 1] + mid + ends[middle - 1 :])
        other = [a_one_other] + [routes.sibling(v) for v in (x_one, y_one)]
        sums = jnp.sum(lax.all_to_all(per_device(partial), BOTH, 0, 0, tiled=True), axis=0)
        low_one, high_one, a_two, third, sums = after([low_one, high_one, a_two, third, sums], other)
        other = other + [routes.sibling(v) for v in (low_one, high_one)]
        pieces = [a_one, x_one, y_one, low_one, high_one], other, own[:2]
        qkv_w, out_w = weights_of([w_qkv, w_out], pieces, chips, rows, True)
        x_two, y_two = routes.swap(a_two, 1), routes.swap(a_two, 2)
        ends = routes.along(third, *near)
        (a_two_sent,) = after([a_two], other)
        a_two_other = routes.sibling(a_two_sent)
        qkv = project_qkv(qkv_w, pos, normed)
        qkv, ends, third = after([qkv, ends, third])
        mid = routes.along(third, middle)
        own += [routes.sibling(w) for w in after([w_up, w_down], qkv)]
        mixed = attend(qkv.reshape(images, padded, 3 * width), seq, width)
        x_two, y_two, ends, mid, mixed, fourth, a_two_other, own = after(
            [x_two, y_two, ends, mid, mixed, fourth, a_two_other, own]
        )
        a_three = joined(ends[: middle - 1] + mid + ends[middle - 1 :])
        mixed = mixed.reshape(images * padded, width)
        low_two, high_two = routes.swap(x_two[:half], 2), routes.swap(y_two[half:], 1)
        early = routes.along(fourth, *range(1, middle))
        other = [a_two_other] + [routes.sibling(v) for v in (x_two, y_two)]
        fourth, other = after([fourth, other])
        last = routes.along(fourth, *range(middle + 1, chips))
        resid, normed_two = project_out(out_w, pos, mixed, tokens, ln2_gain)
        low_two, high_two, early, other, normed_two, a_three, fourth = after(
            [low_two, high_two, early, other, normed_two, a_three, fourth]
        )
        other = other + [routes.sibling(v) for v in (low_two, high_two)]
        pieces = [a_two, x_two, y_two, low_two, high_two], other, own[2:3]
        (up_w,) = weights_of([w_up], pieces, chips, rows, True)
        x_three, y_three = routes.swap(a_three, 1), routes.swap(a_three, 2)
        mid = routes.along(fourth, middle)
        a_three_sent, other = after([a_three, other])
        a_three_other = routes.sibling(a_three_sent)
        active = project_up(up_w, pos, normed_two)
        active, mid, a_three_other, x_three, y_three, last = after(
            [active, mid, a_three_other, x_three, y_three, last]
        )
        diagonal = early + mid + last
        other = [a_three_other] + [routes.sibling(v) for v in [x_three, y_three] + diagonal]
        pieces = [a_three, x_three, y_three] + diagonal, other, own[3:]
        (down_w,) = weights_of([w_down], pieces, chips, w_down.shape[0], False)
    else:
        counts, partial = counting(named)
        sums = jnp.sum(lax.all_to_all(per_device(partial), BOTH, 0, 0, tiled=True), axis=0)
        qkv_w, out_w, up_w, down_w = [whole_weight(w, fsdp) for w in (w_qkv, w_out, w_up, w_down)]
        qkv = project_qkv(qkv_w, pos, normed).reshape(images, padded, 3 * width)
        mixed = attend(qkv, seq, width).reshape(images * padded, width)
        resid, normed_two = project_out(out_w, pos, mixed, tokens, ln2_gain)
        active = project_up(up_w, pos, normed_two)
    pooled = project_down(down_w, pos, active, resid, post_gain, sums, images, seq, devices)
    every = lax.all_to_all(pooled, BOTH, 0, 0, tiled=True).reshape(every_image, -1)
    table_new, accum_new, content_grad, proj_grad = update(
        pos, every, w_proj, counts, table[0], accum[0], images, width // devices
    )
    return table_new[None], accum_new[None], content_grad, proj_grad


def solution(mesh):
    rows = P(("grp", "fsdp"), None)
    deep = P(("grp", "fsdp"), None, None)
    split = P("fsdp", None)
    placed = (
        deep, P(), split, split, P(), split, split, P(), P(), deep, deep, P(), rows, P(("grp", "fsdp")),
    )
    return jax.shard_map(
        on_device, mesh=mesh, in_specs=placed, out_specs=(deep, deep, rows, rows), check_vma=False
    )
```

```python
import functools
import math

import jax
import jax.numpy as jnp
from jax import lax
from jax.experimental import pallas as pl
from jax.experimental.pallas import tpu as pltpu
from jax.sharding import PartitionSpec as P

HEADS = 16
LOOK_IMG = 64
CORES = 2
LANES = 128
MIB = 1 << 20
ROOM = 58

epsilon = 1e-06
learn_rate = 0.5
bf16 = jnp.bfloat16
f32 = jnp.float32
BOTH = ("grp", "fsdp")

VMEM = pl.BlockSpec(memory_space=pltpu.VMEM)
SMEM = pl.BlockSpec(memory_space=pltpu.SMEM)
ANY = pl.BlockSpec(memory_space=pl.ANY)
SHORT = pl.CostEstimate(flops=1, bytes_accessed=1, transcendentals=0)


def norm_rows(values, gain):
    center = jnp.mean(values, axis=-1, keepdims=True)
    shifted = values - center
    spread = jnp.mean(shifted * shifted, axis=-1, keepdims=True)
    return shifted * lax.rsqrt(spread + epsilon) * gain


def after(values, *others):
    return lax.optimization_barrier((tuple(values), tuple(others)))[0]


class Routes:
    def __init__(self, grp, fsdp):
        self.grp, self.fsdp, self.chips = grp, fsdp, fsdp // CORES

    def moved(self, value, target):
        pairs = []
        for index in range(self.grp * self.fsdp):
            plane, rest = divmod(index, self.fsdp)
            chip, core = divmod(rest, CORES)
            there = target(plane, chip, core)
            pairs.append((index, (there[0] * self.chips + there[1]) * CORES + there[2]))
        return lax.ppermute(value, BOTH, pairs)

    def along(self, value, *steps):
        return [
            self.moved(value, lambda g, c, k, step=step: (g, (c - step) % self.chips, k))
            for step in steps
        ]

    def swap(self, value, bit):
        return self.moved(value, lambda g, c, k: (g ^ bit, c, k))

    def sibling(self, value):
        return self.moved(value, lambda g, c, k: (g, c, k ^ 1))


def quarter_of(shards, plane):
    return jnp.concatenate(
        [
            lax.dynamic_slice_in_dim(s, plane * (s.shape[1] // 4), s.shape[1] // 4, axis=1)
            for s in shards
        ],
        axis=1,
    )


def piece_plan(chips, rows, wide, offset, halved):
    plan = []
    half = (chips - 1) * rows // 2
    for turn in range(3):
        for step in range(1, chips):
            for side in range(2):
                plan.append((1 + turn, (step - 1) * rows, rows, offset, side, step, 0, turn))
    for step in range(1, chips):
        for side in range(2):
            if not halved:
                plan.append((3 + step, 0, rows, offset, side, step, 0, 3))
                continue
            first, last = (step - 1) * rows, step * rows
            for buffer, low, high, base in ((4, 0, half, 0), (5, half, 2 * half, half)):
                start, stop = max(first, low), min(last, high)
                if start < stop:
                    plan.append(
                        (buffer, start - base, stop - start, offset, side, step, start - first, 3)
                    )
    return plan


class Weight:
    def __init__(self, shape, wide, pieces, plan, chips, rows):
        self.shape, self.wide, self.pieces = shape, wide, pieces
        self.plan, self.chips, self.rows = plan, chips, rows

    @property
    def count(self):
        return len(self.pieces)

    @property
    def copies(self):
        return 4 if self.plan is None else 8 + len(self.plan)

    def quarter(self, pos, turn):
        return turn if self.plan is None else pos[0] ^ turn

    def moves(self, refs, whole, sems, pos):
        groups = [[], [], [], []]
        number, half = 0, self.count // 2

        def go(source, target, turn):
            nonlocal number
            groups[turn].append(pltpu.make_async_copy(source, target, sems.at[number]))
            number += 1

        for turn in range(4):
            columns = pl.ds(pl.multiple_of(self.quarter(pos, turn) * self.wide, LANES), self.wide)
            if self.plan is None:
                go(refs[0].at[:, columns], whole.at[turn], turn)
                continue
            chip, core = pos[1], pos[2]
            for side in range(2):
                row = pl.multiple_of((chip * CORES + (core ^ side)) * self.rows, self.rows)
                go(refs[side * half].at[:, columns], whole.at[turn, pl.ds(row, self.rows), :], turn)
            for buffer, low, count, column, side, step, inner, own in self.plan:
                if own != turn:
                    continue
                there = lax.rem(chip + step, self.chips)
                row = (there * CORES + (core ^ side)) * self.rows + inner
                row = pl.multiple_of(row, math.gcd(self.rows, inner) if inner else self.rows)
                go(
                    refs[side * half + buffer].at[pl.ds(low, count), pl.ds(column, self.wide)],
                    whole.at[turn, pl.ds(row, count), :],
                    turn,
                )
        return groups


def weights_of(shards, pieces, chips, rows, halved):
    found, offset = [], 0
    sent, other, other_own = pieces
    for number, shard in enumerate(shards):
        wide = shard.shape[1] // 4
        found.append(
            Weight(
                (rows * chips * CORES, shard.shape[1]), wide,
                [shard] + sent + [other_own[number]] + other,
                piece_plan(chips, rows, wide, offset, halved), chips, rows,
            )
        )
        offset += wide
    return found


def whole_weight(shard, fsdp):
    full = lax.all_gather(shard, "fsdp", axis=0, tiled=True)
    return Weight(full.shape, shard.shape[1] // 4, [full], None, fsdp // CORES, shard.shape[0])


def call_with_weight(weight, body, pos, inputs, outs, scratch, room, name):
    n_in, n_out = len(inputs), len(outs)

    def kernel(*refs):
        pos_ref, refs = refs[0], refs[1:]
        pieces, refs = refs[: weight.count], refs[weight.count :]
        sources, refs = refs[:n_in], refs[n_in:]
        targets, refs = refs[:n_out], refs[n_out:]
        whole, sems, in_sems, out_sem = refs[:4]
        ins, refs = refs[4 : 4 + n_in], refs[4 + n_in :]
        held, rest = refs[:n_out], refs[n_out:]
        first = [
            pltpu.make_async_copy(source, target, in_sems.at[number])
            for number, (source, target) in enumerate(zip(sources, ins, strict=True))
        ]
        for copy in first:
            copy.start()
        groups = weight.moves(pieces, whole, sems, pos_ref)
        for copy in groups[0]:
            copy.start()
        sent = []

        def each_turn(work):
            for copy in first:
                copy.wait()
            for turn in range(4):
                for copy in groups[turn]:
                    copy.wait()
                for copy in groups[turn + 1] if turn < 3 else []:
                    copy.start()
                left = pl.multiple_of(weight.quarter(pos_ref, turn) * weight.wide, LANES)
                work(turn, whole.at[turn], pl.ds(left, weight.wide))

        def flush(number, *at):
            copy = pltpu.make_async_copy(
                held[number].at[at], targets[number].at[at], out_sem.at[len(sent)]
            )
            copy.start()
            sent.append(copy)

        body(ins, held, rest, each_turn, flush)
        for copy in sent:
            copy.wait()

    return pl.pallas_call(
        kernel,
        out_shape=outs,
        in_specs=[SMEM] + [ANY] * (weight.count + n_in),
        out_specs=[ANY] * n_out,
        scratch_shapes=[
            pltpu.VMEM((4, weight.shape[0], weight.wide), bf16),
            pltpu.SemaphoreType.DMA((weight.copies,)),
            pltpu.SemaphoreType.DMA((n_in,)),
            pltpu.SemaphoreType.DMA((8,)),
        ]
        + [pltpu.VMEM(v.shape, v.dtype) for v in inputs]
        + [pltpu.VMEM(v.shape, v.dtype) for v in outs]
        + list(scratch),
        compiler_params=pltpu.CompilerParams(vmem_limit_bytes=room * MIB),
        cost_estimate=SHORT,
        name=name,
    )(pos, *weight.pieces, *inputs)


def dot32(left, right):
    return jnp.dot(left, right, preferred_element_type=f32)


def prepare(hidden, gain, padded):
    images, seq, width = hidden.shape
    full = seq // 16

    def kernel(hidden_ref, gain_ref, tokens, normed):
        for image in range(images):
            for number in range(padded // 16):
                at = slice(image * padded + number * 16, image * padded + (number + 1) * 16)
                if number < full:
                    part = hidden_ref[image, number * 16 : (number + 1) * 16, :]
                    tokens[at, :] = part
                    rows = part.astype(f32)
                else:
                    index = lax.broadcasted_iota(jnp.int32, (16, 1), 0)
                    rows = jnp.zeros((16, width), f32)
                    for extra in range(seq - number * 16):
                        row = hidden_ref[image, pl.ds(number * 16 + extra, 1), :].astype(f32)
                        rows = jnp.where(index == extra, row, rows)
                    tokens[at, :] = rows.astype(bf16)
                normed[at, :] = norm_rows(rows, gain_ref[...]).astype(bf16)

    shape = jax.ShapeDtypeStruct((images * padded, width), bf16)
    return pl.pallas_call(
        kernel, out_shape=[shape, shape], in_specs=[VMEM, VMEM], out_specs=[VMEM, VMEM],
        compiler_params=pltpu.CompilerParams(vmem_limit_bytes=16 * MIB),
        cost_estimate=SHORT, name="prepare",
    )(hidden, gain.reshape(1, -1))


def project_qkv(weight, pos, normed):
    def body(ins, outs, scratch, each_turn, flush):
        def quarter(turn, part, columns):
            outs[0][:, columns] = dot32(ins[0][...], part[...]).astype(bf16)
            flush(0, slice(None), columns)

        each_turn(quarter)

    out = jax.ShapeDtypeStruct((normed.shape[0], weight.shape[1]), bf16)
    return call_with_weight(weight, body, pos, [normed], [out], [], ROOM, "project_qkv")[0]


def attend(qkv, seq, width):
    images, padded = qkv.shape[:2]
    head_dim = width // HEADS
    per = LANES // head_dim
    wide = math.gcd(width, 4 * LANES)
    blocks = width // wide
    factor = 1.0 / (math.sqrt(head_dim) * math.log(2.0))

    def kernel(query, keys, values, out):
        lane = lax.broadcasted_iota(jnp.int32, (1, LANES), 1)
        column = lax.broadcasted_iota(jnp.int32, (1, padded), 1)
        for pair in range(wide // LANES):
            at = slice(pair * LANES, (pair + 1) * LANES)
            q, k, v = query[0, :, at], keys[0, :, at], values[0, :, at]
            beside = jnp.concatenate([v, jnp.ones_like(v)], axis=1)
            total = None
            for head in range(per):
                own = (lane // head_dim) == head
                scores = lax.dot_general(
                    jnp.where(own, q, jnp.zeros_like(q)), k,
                    (((1,), (1,)), ((), ())), preferred_element_type=f32,
                )
                scores = jnp.where(column < seq, scores, -1e30)
                top = jnp.max(scores, axis=-1, keepdims=True)
                probs = jnp.exp2((scores - top) * factor).astype(bf16)
                both = dot32(probs, beside)
                mixed = both[:, :LANES] / both[:, LANES:]
                total = mixed if total is None else jnp.where(own, mixed, total)
            out[0, :, at] = total.astype(bf16)

    spec = lambda shift: pl.BlockSpec((1, padded, wide), lambda i, h: (i, 0, h + shift * blocks))
    return pl.pallas_call(
        kernel,
        grid=(images, blocks),
        out_shape=jax.ShapeDtypeStruct((images, padded, width), bf16),
        in_specs=[spec(0), spec(1), spec(2)],
        out_specs=spec(0),
        compiler_params=pltpu.CompilerParams(vmem_limit_bytes=16 * MIB),
        cost_estimate=SHORT,
        name="attend",
    )(qkv, qkv, qkv)


def project_out(weight, pos, mixed, tokens, gain):
    rows, width = mixed.shape

    def body(ins, outs, scratch, each_turn, flush):
        mixed_ref, tokens_ref, gain_ref = ins
        resid, normed = outs

        def quarter(turn, part, columns):
            product = dot32(mixed_ref[...], part[...])
            resid[:, columns] = (tokens_ref[:, columns].astype(f32) + product).astype(bf16)

        each_turn(quarter)
        flush(0, slice(None), slice(None))
        for number in range(rows // 16):
            at = slice(number * 16, (number + 1) * 16)
            normed[at, :] = norm_rows(resid[at, :].astype(f32), gain_ref[...]).astype(bf16)
        flush(1, slice(None), slice(None))

    shape = jax.ShapeDtypeStruct((rows, width), bf16)
    return call_with_weight(
        weight, body, pos, [mixed, tokens, gain.reshape(1, -1)], [shape, shape], [], 12, "project_out"
    )


def gelu(values):
    return 0.5 * values * (1.0 + lax.erf(values * math.sqrt(0.5)))


def project_up(weight, pos, normed):
    size = math.gcd(weight.wide, 512)

    def body(ins, outs, scratch, each_turn, flush):
        def quarter(turn, part, columns):
            for number in range(weight.wide // size):
                left = pl.multiple_of(columns.start + number * size, LANES)
                upward = dot32(ins[0][...], part[:, number * size : (number + 1) * size])
                outs[0][:, pl.ds(left, size)] = gelu(upward).astype(bf16)
            flush(0, slice(None), columns)

        each_turn(quarter)

    out = jax.ShapeDtypeStruct((normed.shape[0], weight.shape[1]), bf16)
    return call_with_weight(weight, body, pos, [normed], [out], [], 20, "project_up")[0]


def thirds(values):
    first = values.astype(bf16)
    left = values - first.astype(f32)
    second = left.astype(bf16)
    return first, second, (left - second.astype(f32)).astype(bf16)


def project_down(weight, pos, active, resid, gain, sums, images, seq, devices):
    rows, width = resid.shape
    padded = rows // images

    def body(ins, outs, scratch, each_turn, flush):
        active_ref, resid_ref, gain_ref, sums_ref = ins
        (final,) = scratch
        (pooled,) = outs

        def quarter(turn, part, columns):
            product = dot32(active_ref[...], part[...])
            final[:, columns] = resid_ref[:, columns].astype(f32) + product

        each_turn(quarter)
        split = [part.astype(f32) for part in thirds(sums_ref[...])]
        step = 16
        for image in range(images):
            total = jnp.zeros((step, width), f32)
            for number in range(padded // step):
                at = slice(image * padded + number * step, image * padded + (number + 1) * step)
                posted = norm_rows(final[at, :], gain_ref[...])
                if (number + 1) * step > seq:
                    row = lax.broadcasted_iota(jnp.int32, (step, 1), 0) + number * step
                    posted = jnp.where(row < seq, posted, 0.0)
                total = total + posted
            mean = jnp.sum(total, axis=0, keepdims=True) / seq
            at = slice(image, image + 1)
            row = jnp.concatenate([mean] + [part[at, :] for part in split], axis=1).astype(bf16)
            for device in range(devices):
                pooled[device, at, :] = row
        flush(0, slice(None), slice(None), slice(None))

    return call_with_weight(
        weight, body, pos, [active, resid, gain.reshape(1, -1), sums],
        [jax.ShapeDtypeStruct((devices, images, width + 3 * sums.shape[1]), bf16)],
        [pltpu.VMEM((rows, width), f32)], 26, "project_down",
    )[0]


def update(pos, every, proj, named, table, accum, images, share):
    rows, width = table.shape
    every_image, depth = every.shape[0], proj.shape[0]
    blocks = rows // LANES
    per = 8 if blocks % 8 == 0 else 1
    side = max(share, LANES)
    over = (((0,), (0,)), ((), ()))

    def kernel(pos_ref, every_ref, proj_ref, named_ref, table_ref, accum_ref,
               table_out, accum_out, content_out, proj_out, units, grads, square):
        @pl.when(pl.program_id(0) == 0)
        def _():
            content = dot32(every_ref[:, :depth], proj_ref[...])
            scale = lax.rsqrt(jnp.mean(content * content, axis=-1, keepdims=True) + epsilon)
            unit = content * scale
            for number, part in enumerate(thirds(unit)):
                units[:, number * width : (number + 1) * width] = part
            units[:, 3 * width :] = jnp.ones((every_image, width), bf16)
            sums = sum(
                every_ref[:, depth + part * width : depth + (part + 1) * width].astype(f32)
                for part in range(3)
            )
            grad_unit = LOOK_IMG * unit - sums
            inner = jnp.mean(grad_unit * unit, axis=-1, keepdims=True)
            grad = scale * (grad_unit - unit * inner)
            grads[...] = grad
            me = pos_ref[3]
            for image in range(images):
                content_out[image : image + 1, :] = grads[pl.ds(me * images + image, 1), :]
            column = me * share
            block = pl.multiple_of((column // side) * side, side)
            mine = every_ref[:, pl.ds(block, side)]
            total = None
            for part in thirds(grad):
                product = lax.dot_general(mine, part, over, preferred_element_type=f32)
                total = product if total is None else total + product
            square[...] = total
            unit_rows = math.gcd(share, side)
            proj_out[...] = square[pl.ds(pl.multiple_of(column - block, unit_rows), share), :]

        for number in range(per):
            at = slice(number * LANES, (number + 1) * LANES)
            found = dot32(named_ref[at, :], units[...])
            taken = found[:, :width] + found[:, width : 2 * width] + found[:, 2 * width : 3 * width]
            old = table_ref[at, :]
            grad_rows = found[:, 3 * width :] * old - taken
            grown = accum_ref[at, :] + grad_rows * grad_rows
            accum_out[at, :] = grown
            table_out[at, :] = old - learn_rate * grad_rows / jnp.sqrt(grown)

    whole = lambda shape: pl.BlockSpec(shape, lambda i: (0,) * len(shape))
    strip = pl.BlockSpec((per * LANES, width), lambda i: (i, 0))
    return pl.pallas_call(
        kernel,
        grid=(blocks // per,),
        out_shape=[
            jax.ShapeDtypeStruct(table.shape, f32),
            jax.ShapeDtypeStruct(table.shape, f32),
            jax.ShapeDtypeStruct((images, width), f32),
            jax.ShapeDtypeStruct((share, width), f32),
        ],
        in_specs=[
            SMEM, whole(every.shape), whole(proj.shape),
            pl.BlockSpec((per * LANES, every_image), lambda i: (i, 0)), strip, strip,
        ],
        out_specs=[strip, strip, whole((images, width)), whole((share, width))],
        scratch_shapes=[
            pltpu.VMEM((every_image, 4 * width), bf16),
            pltpu.VMEM((every_image, width), f32),
            pltpu.VMEM((side, width), f32),
        ],
        compiler_params=pltpu.CompilerParams(vmem_limit_bytes=ROOM * MIB),
        name="update",
    )(pos, every, proj, named, table, accum)


def broadcast_all(value, devices):
    return lax.all_to_all(
        jnp.broadcast_to(value[None], (devices,) + value.shape), BOTH, 0, 0, tiled=True
    )


def count_rows(named, table, mine, images):
    rows_dev = table.shape[0]
    tables = named[:, 0].reshape(images, LOOK_IMG)
    spots = named[:, 1].reshape(images, LOOK_IMG)
    high = jnp.where(tables == mine, spots // LANES, -1)
    left = (high[:, :, None] == jnp.arange(rows_dev // LANES)[None, None, :]).astype(bf16)
    right = ((spots % LANES)[:, :, None] == jnp.arange(LANES)[None, None, :]).astype(bf16)
    counts = jnp.einsum("ilh,ilr->ihr", left, right, preferred_element_type=f32)
    partial = jnp.dot(
        counts.reshape(images, rows_dev), table,
        precision=lax.Precision.HIGHEST, preferred_element_type=f32,
    )
    return jnp.transpose(counts, (1, 2, 0)).reshape(rows_dev, images).astype(bf16), partial


def on_device(
    hidden, ln1_gain, w_qkv, w_out, ln2_gain, w_up, w_down, post_gain, w_proj,
    table, accum, place, lookup_table, lookup_row,
):
    images, seq, width = hidden.shape
    grp, fsdp = lax.axis_size("grp"), lax.axis_size("fsdp")
    devices = grp * fsdp
    plane, spot = lax.axis_index("grp"), lax.axis_index("fsdp")
    me = plane * fsdp + spot
    pos = jnp.stack([plane, spot // CORES, spot % CORES, me]).astype(jnp.int32)

    rows = w_qkv.shape[0]
    routes = Routes(grp, fsdp)
    chips = routes.chips
    simple = grp == 4 and fsdp % CORES == 0 and chips % 2 == 0 and rows % LANES == 0
    joined = lambda parts: jnp.concatenate(parts, axis=0)
    half = (chips - 1) * rows // 2
    middle = chips // 2
    near = [step for step in range(1, chips) if step != middle]
    padded = -(-seq // 16) * 16
    tokens, normed = prepare(hidden, ln1_gain, padded)
    if simple:
        first = quarter_of([w_qkv, w_out], plane)
        ends = routes.along(first, *near)
        mid = routes.along(first, middle)
        own = [routes.sibling(w) for w in after([w_qkv, w_out], first)]
        a_one = joined(ends[: middle - 1] + mid + ends[middle - 1 :])
        second, third, fourth = (
            quarter_of([w_up], plane), quarter_of([w_down], plane), quarter_of([w_down], plane ^ 3),
        )

    rows_dev, proj_width = table.shape[1:]
    every_image = images * devices
    my_table = jnp.sum(jnp.where(place == me, jnp.arange(place.shape[0], dtype=jnp.int32), 0))
    named = broadcast_all(jnp.stack([lookup_table[:, 0], lookup_row]), devices)
    per_device = lambda v: v.reshape(devices, images, proj_width)
    counting = functools.partial(count_rows, table=table[0], mine=my_table, images=every_image)

    if simple:
        a_one, second, third, fourth, named = after([a_one, second, third, fourth, named], own, normed)
        x_one, y_one = routes.swap(a_one, 1), routes.swap(a_one, 2)
        ends = routes.along(second, *near)
        a_one_other = routes.sibling(a_one)
        counts, partial = counting(named)
        x_one, y_one, second, counts, partial = after(
            [x_one, y_one, second, counts, partial], ends, a_one_other
        )
        low_one, high_one = routes.swap(x_one[:half], 2), routes.swap(y_one[half:], 1)
        mid = routes.along(second, middle)
        a_two = joined(ends[: middle - 1] + mid + ends[middle - 1 :])
        other = [a_one_other] + [routes.sibling(v) for v in (x_one, y_one)]
        sums = jnp.sum(lax.all_to_all(per_device(partial), BOTH, 0, 0, tiled=True), axis=0)
        low_one, high_one, a_two, third, sums = after([low_one, high_one, a_two, third, sums], other)
        other = other + [routes.sibling(v) for v in (low_one, high_one)]
        pieces = [a_one, x_one, y_one, low_one, high_one], other, own[:2]
        qkv_w, out_w = weights_of([w_qkv, w_out], pieces, chips, rows, True)
        x_two, y_two = routes.swap(a_two, 1), routes.swap(a_two, 2)
        ends = routes.along(third, *near)
        (a_two_sent,) = after([a_two], other)
        a_two_other = routes.sibling(a_two_sent)
        qkv = project_qkv(qkv_w, pos, normed)
        qkv, ends, third = after([qkv, ends, third])
        mid = routes.along(third, middle)
        own += [routes.sibling(w) for w in after([w_up, w_down], qkv)]
        mixed = attend(qkv.reshape(images, padded, 3 * width), seq, width)
        x_two, y_two, ends, mid, mixed, fourth, a_two_other, own = after(
            [x_two, y_two, ends, mid, mixed, fourth, a_two_other, own]
        )
        a_three = joined(ends[: middle - 1] + mid + ends[middle - 1 :])
        mixed = mixed.reshape(images * padded, width)
        low_two, high_two = routes.swap(x_two[:half], 2), routes.swap(y_two[half:], 1)
        early = routes.along(fourth, *range(1, middle))
        other = [a_two_other] + [routes.sibling(v) for v in (x_two, y_two)]
        fourth, other = after([fourth, other])
        last = routes.along(fourth, *range(middle + 1, chips))
        resid, normed_two = project_out(out_w, pos, mixed, tokens, ln2_gain)
        low_two, high_two, early, other, normed_two, a_three, fourth = after(
            [low_two, high_two, early, other, normed_two, a_three, fourth]
        )
        other = other + [routes.sibling(v) for v in (low_two, high_two)]
        pieces = [a_two, x_two, y_two, low_two, high_two], other, own[2:3]
        (up_w,) = weights_of([w_up], pieces, chips, rows, True)
        x_three, y_three = routes.swap(a_three, 1), routes.swap(a_three, 2)
        mid = routes.along(fourth, middle)
        a_three_sent, other = after([a_three, other])
        a_three_other = routes.sibling(a_three_sent)
        active = project_up(up_w, pos, normed_two)
        active, mid, a_three_other, x_three, y_three, last = after(
            [active, mid, a_three_other, x_three, y_three, last]
        )
        diagonal = early + mid + last
        other = [a_three_other] + [routes.sibling(v) for v in [x_three, y_three] + diagonal]
        pieces = [a_three, x_three, y_three] + diagonal, other, own[3:]
        (down_w,) = weights_of([w_down], pieces, chips, w_down.shape[0], False)
    else:
        counts, partial = counting(named)
        sums = jnp.sum(lax.all_to_all(per_device(partial), BOTH, 0, 0, tiled=True), axis=0)
        qkv_w, out_w, up_w, down_w = [whole_weight(w, fsdp) for w in (w_qkv, w_out, w_up, w_down)]
        qkv = project_qkv(qkv_w, pos, normed).reshape(images, padded, 3 * width)
        mixed = attend(qkv, seq, width).reshape(images * padded, width)
        resid, normed_two = project_out(out_w, pos, mixed, tokens, ln2_gain)
        active = project_up(up_w, pos, normed_two)
    pooled = project_down(down_w, pos, active, resid, post_gain, sums, images, seq, devices)
    every = lax.all_to_all(pooled, BOTH, 0, 0, tiled=True).reshape(every_image, -1)
    table_new, accum_new, content_grad, proj_grad = update(
        pos, every, w_proj, counts, table[0], accum[0], images, width // devices
    )
    return table_new[None], accum_new[None], content_grad, proj_grad


def solution(mesh):
    rows = P(("grp", "fsdp"), None)
    deep = P(("grp", "fsdp"), None, None)
    split = P("fsdp", None)
    placed = (
        deep, P(), split, split, P(), split, split, P(), P(), deep, deep, P(), rows, P(("grp", "fsdp")),
    )
    return jax.shard_map(
        on_device, mesh=mesh, in_specs=placed, out_specs=(deep, deep, rows, rows), check_vma=False
    )
```
